32 devices in a mesh: tm: 4 (over z), lat: 4 (over y, core), lon: 2 (over x).
Axes of the slice: x: 2, y: 2, z: 4, core: 2. Of those that a mesh axis runs over, the one named last changes fastest.
Arguments:
- depth_class: int32 [544, 768], P('lat', 'lon'), may hold values from 0 to 31
- ocean_mask: int32 [544, 768], P('lat', 'lon'), may hold values 0 or 1
- depth_levels: float32 [32], replicated, may hold values from 0.1 to 1
- drag: float32 [544, 768], P('lat', 'lon'), may hold values from 0.0005 to 0.02
- tide_force: float32 [2, 544, 768], P(None, 'lat', 'lon'), may hold values from -6 to 6
- forward_flow: float32 [4, 544, 768], P(None, 'lat', 'lon'), may hold values from -6 to 6
- guess: float32 [4, 3, 544, 768], P('tm', None, 'lat', 'lon'), may hold values from -4 to 4
Outputs:
- final_state: float32 [4, 3, 544, 768], P('tm', None, 'lat', 'lon')
- drag_gradient: float32 [544, 768], P('lat', 'lon')
The draws below stay inside these ranges and needn't reach their ends.
Inputs may be any that keep to these rules, and one draw needn't show every extreme that they name: `depth_class`: index into depth_levels.
All inputs are finite; a program needn't handle non-finite values. No bound on the sum of `ocean_mask` on one device may be relied on, other than what follows from the above.
Results may differ from the reference program's by a relative error of at most 0.00002.
Values sent between devices are 32-bit elements; how exact they have to be, the bound alone decides.
A program may use at most 64 MiB of HBM per device.

```python
import math
import jax
import jax.numpy as jnp

STEPS = 16
SWEEPS = 2
DCLASS = 32
NY = 544
NX = 768
N_TM = 4


def set_ends(array, rng, smallest, top_value):
    shape = array.shape
    place = [jax.random.randint(jax.random.fold_in(rng, axis), (), 0, shape[axis]) for axis in range(len(shape))]
    array = array.at[tuple(place)].set(smallest)
    longest = shape.index(max(shape))
    place[longest] = (place[longest] + 1) % shape[longest]
    return array.at[tuple(place)].set(top_value)


def levels(key, dims, pieces, least, largest):
    level, own = 1.0, jax.random.fold_in(key, 6)
    for position, parts in pieces:
        heights = jnp.exp(jax.random.uniform(jax.random.fold_in(own, position), (parts,), jnp.float32, least / len(pieces), largest / len(pieces)))
        level = level * jnp.repeat(heights, dims[position] // parts).reshape([-1 if axis == position else 1 for axis in range(len(dims))])
    return level


def centred(own_key, extent, width, reach, split=(), held_as=jnp.bfloat16):
    result = width * jax.random.normal(own_key, extent, jnp.float32)
    if split:
        result = result * levels(own_key, extent, split, -0.22, 0.18)
    return jnp.clip(result, -reach, reach).astype(held_as)


def setup_inputs(seed: int = 0) -> dict:
    splits = jax.random.split(jax.random.key(seed), 8)
    return {
        "depth_class": set_ends(jax.random.randint(splits[0], (NY, NX), 0, DCLASS), jax.random.fold_in(splits[0], 1), 0, DCLASS - 1).astype(jnp.int32),
        "ocean_mask": set_ends((jax.random.randint(splits[1], (NY, NX), 0, 10) < 7).astype(jnp.int32), jax.random.fold_in(splits[1], 1), 0, 1),
        "depth_levels": jnp.clip(jnp.exp(jax.random.uniform(splits[2], (DCLASS,), jnp.float32, math.log(0.1), math.log(1.0))), 0.1, 1.0),
        "drag": jnp.clip(jnp.exp(math.log(0.02) - 3.6888794 * jax.random.uniform(splits[3], (NY, NX), jnp.float32) ** levels(splits[3], (NY, NX), ((0, 4), (1, 2)), -0.2, 0.2)), 0.0005, 0.02),
        "tide_force": centred(splits[4], (2, NY, NX), 1.0, 6.0, ((1, 4), (2, 2)), jnp.float32),
        "forward_flow": centred(splits[5], (4, NY, NX), 1.0, 6.0, ((1, 4), (2, 2)), jnp.float32),
        "guess": centred(splits[6], (N_TM, 3, NY, NX), 0.5, 4.0, ((0, 4), (2, 4), (3, 2)), jnp.float32),
    }


def west(x):
    return jnp.roll(x, 1, axis=1)


def east(x):
    return jnp.roll(x, -1, axis=1)


def south(x):
    return jnp.roll(x, 1, axis=0)


def north(x):
    return jnp.roll(x, -1, axis=0)


def reference(depth_class, ocean_mask, depth_levels, drag, tide_force, forward_flow, guess):
    ny = ocean_mask.shape[0]
    classes = jnp.arange(DCLASS, dtype=jnp.int32)
    depth = jnp.sum(jnp.where(depth_class[None] == classes[:, None, None], depth_levels[:, None, None], jnp.float32(0.0)), axis=0)
    rows = jnp.arange(ny, dtype=jnp.int32)
    polar = (rows == 0) | (rows == ny - 1)
    mask = jnp.where(polar[:, None], 0, ocean_mask).astype(jnp.float32)
    hu = 0.5 * (depth + west(depth))
    mu = mask * west(mask)
    du = 1.0 - (drag + west(drag)) / (depth + west(depth))
    hv = 0.5 * (depth + south(depth))
    mv = mask * south(mask)
    dv = 1.0 - (drag + south(drag)) / (depth + south(depth))
    weight = mask / depth
    gain = jnp.stack([mask, mu * du ** STEPS, mv * dv ** STEPS])
    cycle = jnp.float32(N_TM * STEPS)

    def fine(state, slice_index, want):
        elev, zonal, merid = state[0], state[1], state[2]
        term = jnp.zeros_like(elev)
        for sub in range(STEPS):
            count = slice_index * STEPS + sub + 1
            angle = jnp.float32(2.0 * math.pi) * jnp.float32(count) / cycle
            cosine, sine = jnp.cos(angle), jnp.sin(angle)
            zonal = mu * (du * zonal - 0.7 * (elev - west(elev)))
            merid = mv * (dv * merid - 0.7 * (elev - south(elev)))
            flux_u = hu * zonal
            flux_v = hv * merid
            spread = (east(flux_u) - flux_u) + (north(flux_v) - flux_v)
            source = tide_force[0] * cosine + tide_force[1] * sine
            elev = mask * (elev - 0.6 * spread + source)
            if want:
                flow_u = forward_flow[0] * cosine + forward_flow[1] * sine
                flow_v = forward_flow[2] * cosine + forward_flow[3] * sine
                u_mid = 0.5 * (zonal + east(zonal))
                v_mid = 0.5 * (merid + north(merid))
                term = term + weight * (flow_u * u_mid + flow_v * v_mid)
        return jnp.stack([elev, zonal, merid]), term

    bounds = [guess[k] for k in range(N_TM)]
    total = jnp.zeros_like(depth)
    for sweep in range(SWEEPS):
        want = sweep == SWEEPS - 1
        ends = []
        for k in range(N_TM):
            end, term = fine(bounds[k], k, want)
            ends.append(end)
            if want:
                total = total + term
        jumps = [ends[(k - 1) % N_TM] - bounds[k] for k in range(N_TM)]
        change = jumps[0]
        fresh = [bounds[0] + change]
        for k in range(1, N_TM):
            change = jumps[k] + gain * change
            fresh.append(bounds[k] + change)
        bounds = fresh
    final_state = jnp.stack(bounds)
    drag_gradient = total / jnp.float32(N_TM * STEPS)
    return final_state, drag_gradient
```

```python
import functools
import math

import jax
import jax.numpy as jnp
import numpy as np
from jax import lax
from jax.experimental import pallas as pl
from jax.experimental.pallas import tpu as pltpu
from jax.sharding import PartitionSpec as P

STEPS = 16
SWEEPS = 2
DCLASS = 32
WIDE = STEPS
LANES = 128
TILE = 8
SKEW = 2

MESH = pl.DeviceIdType.MESH


def kernel(
    sizes, cls_ref, ocean_ref, lev_ref, drag_ref, force_ref, flow_ref, guess_ref, trig_ref,
    out_ref, grad_ref,
    x_ref, y_ref, st_ref, acc_ref, gain_ref, old_ref, term_ref, east_out, west_out, east_in, west_in,
    c1_ref, cs1_ref, e1_ref, c2_ref, cs2_ref, e2_ref, tot_ref,
    row_send, row_recv, col_send, col_recv,
    c_send, c_recv, e_send, e_recv, t_send, t_recv,
):
    n, n_lat, n_lon = sizes
    rows, cols = ocean_ref.shape
    high, wid = x_ref.shape[1], x_ref.shape[2]
    span = c1_ref.shape[2]
    block = TILE * max(d for d in (1, 2, 3) if (high // TILE) % d == 0)
    count = rows // TILE
    k, lat, lon = lax.axis_index("tm"), lax.axis_index("lat"), lax.axis_index("lon")
    north, south = lax.rem(lat + 1, n_lat), lax.rem(lat + n_lat - 1, n_lat)
    east, west = lax.rem(lon + 1, n_lon), lax.rem(lon + n_lon - 1, n_lon)
    later, sooner = lax.rem(k + 1, n), lax.rem(k + n - 1, n)

    barrier = pltpu.get_barrier_semaphore()
    for axis, spot in (
        ("lat", north), ("lat", south), ("lon", east), ("lon", west), ("tm", later), ("tm", sooner)
    ):
        pl.semaphore_signal(barrier, inc=1, device_id={axis: spot}, device_id_type=MESH)

    mine = pl.ds(WIDE, rows)
    classes = cls_ref[...]
    depth = jnp.zeros((rows, cols), jnp.float32)
    for c in range(DCLASS):
        depth = jnp.where(classes == c, lev_ref[c], depth)
    x_ref[0, mine, :cols] = depth
    line = lat * rows + lax.broadcasted_iota(jnp.int32, (rows, cols), 0)
    polar = (line == 0) | (line == n_lat * rows - 1)
    x_ref[1, mine, :cols] = jnp.where(polar, 0, ocean_ref[...]).astype(jnp.float32)
    x_ref[2, mine, :cols] = drag_ref[...]
    for f in range(2):
        x_ref[3 + f, mine, :cols] = force_ref[f]
    for f in range(3):
        x_ref[5 + f, mine, :cols] = guess_ref[0, f]
    pl.semaphore_wait(barrier, 6)

    def exchange(ref, number, fills):
        fields = len(fills)
        up = pltpu.make_async_remote_copy(
            src_ref=ref.at[:, pl.ds(rows, WIDE), pl.ds(0, span)],
            dst_ref=ref.at[:, pl.ds(0, WIDE), pl.ds(0, span)],
            send_sem=row_send.at[2 * number], recv_sem=row_recv.at[2 * number],
            device_id={"lat": north}, device_id_type=MESH,
        )
        down = pltpu.make_async_remote_copy(
            src_ref=ref.at[:, pl.ds(WIDE, WIDE), pl.ds(0, span)],
            dst_ref=ref.at[:, pl.ds(WIDE + rows, WIDE), pl.ds(0, span)],
            send_sem=row_send.at[2 * number + 1], recv_sem=row_recv.at[2 * number + 1],
            device_id={"lat": south}, device_id_type=MESH,
        )
        up.start()
        down.start()
        up.wait()
        down.wait()
        lane = lax.broadcasted_iota(jnp.int32, (high, LANES), 1)
        last = (cols - WIDE) // LANES * LANES
        inset = cols - WIDE - last
        eastern = western = None
        for f in range(fields):
            e = pltpu.roll(ref[f, :, last : last + LANES], (WIDE * f - inset) % LANES, 1)
            w = pltpu.roll(ref[f, :, :LANES], WIDE * f, 1) if f else ref[f, :, :LANES]
            eastern = jnp.where(lane >= WIDE * f, e, eastern) if f else e
            western = jnp.where(lane >= WIDE * f, w, western) if f else w
        east_out[number] = eastern
        west_out[number] = western
        right = pltpu.make_async_remote_copy(
            src_ref=east_out.at[number], dst_ref=west_in.at[number],
            send_sem=col_send.at[2 * number], recv_sem=col_recv.at[2 * number],
            device_id={"lon": east}, device_id_type=MESH,
        )
        left = pltpu.make_async_remote_copy(
            src_ref=west_out.at[number], dst_ref=east_in.at[number],
            send_sem=col_send.at[2 * number + 1], recv_sem=col_recv.at[2 * number + 1],
            device_id={"lon": west}, device_id_type=MESH,
        )
        right.start()
        left.start()
        right.wait()
        left.wait()
        start = wid - LANES
        own = cols - start
        from_east, from_west = east_in[number], west_in[number]
        for f, fill in enumerate(fills):
            e = pltpu.roll(from_east, (own - WIDE * f) % LANES, 1)
            w = pltpu.roll(from_west, (LANES - WIDE - WIDE * f) % LANES, 1)
            halo = jnp.where(lane < own + WIDE, e, jnp.where(lane >= LANES - WIDE, w, fill))
            if own:
                halo = jnp.where(lane < own, ref[f, :, start:], halo)
            ref[f, :, start:] = halo

    exchange(x_ref, 0, (1.0,) + (0.0,) * 7)

    def below(ref, f, r):
        if r == 0:
            return pltpu.roll(ref[f, :block, :], 1, 0)
        return pltpu.roll(ref[f, r - TILE : r + block, :], 1, 0)[TILE:]

    for r in range(0, high, block):
        here = pl.ds(r, block)
        d, m, g = x_ref[0, here, :], x_ref[1, here, :], x_ref[2, here, :]
        for side, shifted in enumerate(
            (lambda f, v: pltpu.roll(v, 1, 1), lambda f, v: below(x_ref, f, r))
        ):
            both = d + shifted(0, d)
            wet = m * shifted(1, m)
            st_ref[side, here, :] = wet * (1.0 - (g + shifted(2, g)) / both)
            st_ref[2 + side, here, :] = 0.7 * wet
            st_ref[4 + side, here, :] = 0.3 * both
        st_ref[6, here, :] = m
        st_ref[7, here, :] = m * x_ref[3, here, :]
        st_ref[8, here, :] = m * x_ref[4, here, :]
    gain_ref[0] = x_ref[1, mine, :span]
    for side in range(2):
        g = st_ref[side, mine, :span]
        for _ in range(STEPS.bit_length() - 1):
            g = g * g
        gain_ref[1 + side] = g
    acc_ref[...] = jnp.zeros(acc_ref.shape, jnp.float32)

    def sweep(ref, base, want):
        def step(t, nothing):
            cosine = trig_ref[2 * (k * STEPS + t)]
            sine = trig_ref[2 * (k * STEPS + t) + 1]
            carry = None
            for r in reversed(range(0, high, block)):
                here = pl.ds(r, block)
                a = ref[base, here, :]
                p = st_ref[0, here, :] * ref[base + 1, here, :] - st_ref[2, here, :] * (
                    a - pltpu.roll(a, 1, 1)
                )
                q = st_ref[1, here, :] * ref[base + 2, here, :] - st_ref[3, here, :] * (
                    a - below(ref, base, r)
                )
                u = st_ref[4, here, :] * p
                v = st_ref[5, here, :] * q
                if carry is None:
                    v_north = pltpu.roll(v, block - 1, 0)
                else:
                    v_north = pltpu.roll(
                        jnp.concatenate([v, carry], axis=0), block + TILE - 1, 0
                    )[:block]
                carry = v[:TILE]
                spread = (pltpu.roll(u, wid - 1, 1) - u) + (v_north - v)
                ref[base, here, :] = st_ref[6, here, :] * (a - spread) + (
                    st_ref[7, here, :] * cosine + st_ref[8, here, :] * sine
                )
                ref[base + 1, here, :] = p
                ref[base + 2, here, :] = q
                if want:
                    low, top = max(r, WIDE), min(r + block, WIDE + rows + TILE)
                    part = pl.ds(low, top - low)
                    p, q = p[low - r : top - r], q[low - r : top - r]
                    acc_ref[0, part, :] += cosine * p
                    acc_ref[1, part, :] += sine * p
                    acc_ref[2, part, :] += cosine * q
                    acc_ref[3, part, :] += sine * q
            return nothing

        lax.fori_loop(0, STEPS, step, 0)

    def relay(ref, base, number, c_ref, cs_ref, e_ref, want):
        def piece(chunk):
            return pl.ds(pl.multiple_of(chunk * TILE, TILE), TILE)

        def forward(chunk):
            return pltpu.make_async_remote_copy(
                src_ref=cs_ref.at[:, piece(chunk)], dst_ref=c_ref.at[:, piece(chunk)],
                send_sem=c_send.at[number, chunk], recv_sem=c_recv.at[number, chunk],
                device_id={"tm": later}, device_id_type=MESH,
            )

        def back(chunk):
            return pltpu.make_async_remote_copy(
                src_ref=e_ref.at[:, piece(chunk)], dst_ref=e_ref.at[:, piece(chunk)],
                send_sem=e_send.at[number, chunk], recv_sem=e_recv.at[number, chunk],
                device_id={"tm": sooner}, device_id_type=MESH,
            )

        def total(chunk):
            return pltpu.make_async_remote_copy(
                src_ref=tot_ref.at[piece(chunk)], dst_ref=tot_ref.at[piece(chunk)],
                send_sem=t_send.at[chunk], recv_sem=t_recv.at[chunk],
                device_id={"tm": sooner}, device_id_type=MESH,
            )

        @pl.when(k == 0)
        def _():
            c_ref[...] = jnp.zeros(c_ref.shape, jnp.float32)

        @pl.when(k == n - 1)
        def _():
            for f in range(3):
                e_ref[f] = ref[base + f, mine, :span]

        def turn(i, nothing):
            ahead = i - SKEW * k

            @pl.when((ahead >= 0) & (ahead < count))
            def _():
                @pl.when(k > 0)
                def _():
                    forward(ahead).wait_recv()

                here = piece(ahead)
                there = pl.ds(pl.multiple_of(WIDE + ahead * TILE, TILE), TILE)

                @pl.when(k < n - 1)
                def _():
                    for f in range(3):
                        cs_ref[f, here, :] = ref[base + f, there, :span] + gain_ref[f, here, :] * (
                            c_ref[f, here, :] - old_ref[f, here, :]
                        )
                    if want:
                        cs_ref[3, here, :] = c_ref[3, here, :] + term_ref[here, :]
                    forward(ahead).start()

                if want:
                    @pl.when(k == n - 1)
                    def _():
                        tot_ref[here, :] = c_ref[3, here, :] + term_ref[here, :]

            behind = i - SKEW * (n - 1 - k)

            @pl.when((behind >= 0) & (behind < count))
            def _():
                @pl.when(k < n - 1)
                def _():
                    back(behind).wait_recv()

                @pl.when(k > 0)
                def _():
                    back(behind).start()

            if want:
                final = behind - SKEW * (n - 1)

                @pl.when((final >= 0) & (final < count))
                def _():
                    @pl.when(k < n - 1)
                    def _():
                        total(final).wait_recv()

                    @pl.when(k > 0)
                    def _():
                        total(final).start()

            return nothing

        lax.fori_loop(0, count + SKEW * (n - 1) * (2 if want else 1), turn, 0)

        for f in range(3):
            power = e_ref[f]
            for j in range(n - 1):
                power = power * jnp.where(j < k, gain_ref[f], 1.0)
            fresh = c_ref[f] + power
            if want:
                out_ref[0, f] = fresh[:, :cols]
            else:
                old_ref[f] = fresh
                y_ref[f, mine, :span] = fresh

        def sent(chunk, nothing):
            @pl.when(k < n - 1)
            def _():
                forward(chunk).wait_send()

            @pl.when(k > 0)
            def _():
                back(chunk).wait_send()
                if want:
                    total(chunk).wait_send()

            return nothing

        return lambda: lax.fori_loop(0, count, sent, 0)

    for f in range(3):
        old_ref[f] = x_ref[5 + f, mine, :span]
    sweep(x_ref, 5, False)
    finish_first = relay(x_ref, 5, 0, c1_ref, cs1_ref, e1_ref, False)
    exchange(y_ref, 1, (0.0,) * 3)
    sweep(y_ref, 0, True)

    weight = 0.5 * x_ref[1, mine, :span] / x_ref[0, mine, :span]
    term = jnp.zeros((rows, span), jnp.float32)
    for f in range(4):
        if f < 2:
            v = acc_ref[f, mine, :]
            mid = (v + pltpu.roll(v, wid - 1, 1))[:, :span]
        else:
            v = acc_ref[f, pl.ds(WIDE, rows + TILE), :span]
            mid = (v + pltpu.roll(v, rows + TILE - 1, 0))[:rows]
        flow = flow_ref[f]
        if span > cols:
            flow = jnp.concatenate([flow, jnp.zeros((rows, span - cols), jnp.float32)], axis=1)
        term = term + flow * mid
    term_ref[...] = weight * term

    finish_second = relay(y_ref, 0, 1, c2_ref, cs2_ref, e2_ref, True)
    grad_ref[...] = tot_ref[:, :cols] * (1.0 / (n * STEPS))
    finish_first()
    finish_second()


def shards(
    sizes, depth_class, ocean_mask, depth_levels, drag, tide_force, forward_flow, guess
):
    n = sizes[0]
    rows, cols = ocean_mask.shape
    high = rows + 2 * WIDE
    wid = -(-(cols + 2 * WIDE) // LANES) * LANES
    span = -(-cols // LANES) * LANES
    count = rows // TILE
    assert rows % TILE == 0 and rows >= WIDE and wid - LANES <= cols
    counts = np.arange(1, n * STEPS + 1)
    angle = 2.0 * math.pi * counts / (n * STEPS)
    trig = jnp.asarray(np.stack([np.cos(angle), np.sin(angle)], axis=1).reshape(-1), jnp.float32)
    f32 = jnp.float32
    vmem, smem = pl.BlockSpec(memory_space=pltpu.VMEM), pl.BlockSpec(memory_space=pltpu.SMEM)
    dma = pltpu.SemaphoreType.DMA
    return pl.pallas_call(
        functools.partial(kernel, sizes),
        out_shape=(
            jax.ShapeDtypeStruct((1, 3, rows, cols), f32),
            jax.ShapeDtypeStruct((rows, cols), f32),
        ),
        in_specs=[vmem, vmem, smem, vmem, vmem, vmem, vmem, smem],
        out_specs=(vmem, vmem),
        scratch_shapes=[
            pltpu.VMEM((8, high, wid), f32),
            pltpu.VMEM((3, high, wid), f32),
            pltpu.VMEM((9, high, wid), f32),
            pltpu.VMEM((4, high, wid), f32),
            pltpu.VMEM((3, rows, span), f32),
            pltpu.VMEM((3, rows, span), f32),
            pltpu.VMEM((rows, span), f32),
            pltpu.VMEM((2, high, LANES), f32),
            pltpu.VMEM((2, high, LANES), f32),
            pltpu.VMEM((2, high, LANES), f32),
            pltpu.VMEM((2, high, LANES), f32),
            pltpu.VMEM((3, rows, span), f32),
            pltpu.VMEM((3, rows, span), f32),
            pltpu.VMEM((3, rows, span), f32),
            pltpu.VMEM((4, rows, span), f32),
            pltpu.VMEM((4, rows, span), f32),
            pltpu.VMEM((3, rows, span), f32),
            pltpu.VMEM((rows, span), f32),
            dma((4,)), dma((4,)), dma((4,)), dma((4,)),
            dma((2, count)), dma((2, count)), dma((2, count)), dma((2, count)),
            dma((count,)), dma((count,)),
        ],
        compiler_params=pltpu.CompilerParams(
            collective_id=0, has_side_effects=True, vmem_limit_bytes=40 * 1024 * 1024
        ),
        name="parareal",
    )(depth_class, ocean_mask, depth_levels, drag, tide_force, forward_flow, guess, trig)


def solution(mesh):
    sizes = tuple(mesh.shape[axis] for axis in ("tm", "lat", "lon"))
    return jax.shard_map(
        functools.partial(shards, sizes),
        mesh=mesh,
        in_specs=(
            P("lat", "lon"),
            P("lat", "lon"),
            P(),
            P("lat", "lon"),
            P(None, "lat", "lon"),
            P(None, "lat", "lon"),
            P("tm", None, "lat", "lon"),
        ),
        out_specs=(P("tm", None, "lat", "lon"), P("lat", "lon")),
        check_vma=False,
    )
```

```python
import functools
import math

import jax
import jax.numpy as jnp
import numpy as np
from jax import lax
from jax.experimental import pallas as pl
from jax.experimental.pallas import tpu as pltpu
from jax.sharding import PartitionSpec as P

STEPS = 16
SWEEPS = 2
DCLASS = 32
WIDE = STEPS
LANES = 128
TILE = 8
SKEW = 4

MESH = pl.DeviceIdType.MESH


def kernel(
    sizes, cls_hbm, ocean_hbm, lev_hbm, drag_hbm, force_hbm, flow_hbm, guess_hbm, trig_hbm,
    out_ref, grad_ref,
    cls_ref, ocean_ref, lev_ref, drag_ref, force_ref, flow_ref, guess_ref, trig_ref, load_sem,
    x_ref, y_ref, st_ref, acc_ref, gain_ref, old_ref, term_ref, east_out, west_out, east_in, west_in,
    c1_ref, cs1_ref, e1_ref, c2_ref, cs2_ref, e2_ref, part_ref, other_ref, tot_ref,
    row_send, row_recv, col_send, col_recv,
    c_send, c_recv, e_send, e_recv, t_send, t_recv,
):
    n, n_lat, n_lon = sizes
    rows, cols = ocean_ref.shape
    high, wid = x_ref.shape[1], x_ref.shape[2]
    span = c1_ref.shape[2]
    block = TILE * max(d for d in (1, 2, 3) if (high // TILE) % d == 0)
    count = rows // TILE
    k, lat, lon = lax.axis_index("tm"), lax.axis_index("lat"), lax.axis_index("lon")
    north, south = lax.rem(lat + 1, n_lat), lax.rem(lat + n_lat - 1, n_lat)
    east, west = lax.rem(lon + 1, n_lon), lax.rem(lon + n_lon - 1, n_lon)
    later, sooner = lax.rem(k + 1, n), lax.rem(k + n - 1, n)

    loads = [
        pltpu.make_async_copy(source, target, load_sem.at[i])
        for i, (source, target) in enumerate((
            (lev_hbm, lev_ref), (cls_hbm, cls_ref), (ocean_hbm, ocean_ref), (drag_hbm, drag_ref),
            (force_hbm, force_ref), (guess_hbm, guess_ref), (trig_hbm, trig_ref), (flow_hbm, flow_ref),
        ))
    ]
    for load in loads:
        load.start()
    barrier = pltpu.get_barrier_semaphore()
    for axis, spot in (
        ("lat", north), ("lat", south), ("lon", east), ("lon", west), ("tm", later), ("tm", sooner)
    ):
        pl.semaphore_signal(barrier, inc=1, device_id={axis: spot}, device_id_type=MESH)

    mine = pl.ds(WIDE, rows)
    loads[0].wait()
    loads[1].wait()
    classes = cls_ref[...]
    depth = jnp.zeros((rows, cols), jnp.float32)
    for c in range(DCLASS):
        depth = jnp.where(classes == c, lev_ref[c], depth)
    x_ref[0, mine, :cols] = depth
    for load in loads[2:7]:
        load.wait()
    line = lat * rows + lax.broadcasted_iota(jnp.int32, (rows, cols), 0)
    polar = (line == 0) | (line == n_lat * rows - 1)
    x_ref[1, mine, :cols] = jnp.where(polar, 0, ocean_ref[...]).astype(jnp.float32)
    x_ref[2, mine, :cols] = drag_ref[...]
    for f in range(2):
        x_ref[3 + f, mine, :cols] = force_ref[f]
    for f in range(3):
        x_ref[5 + f, mine, :cols] = guess_ref[0, f]
    pl.semaphore_wait(barrier, 6)

    def exchange(ref, number, fills):
        fields = len(fills)
        up = pltpu.make_async_remote_copy(
            src_ref=ref.at[:, pl.ds(rows, WIDE), pl.ds(0, span)],
            dst_ref=ref.at[:, pl.ds(0, WIDE), pl.ds(0, span)],
            send_sem=row_send.at[2 * number], recv_sem=row_recv.at[2 * number],
            device_id={"lat": north}, device_id_type=MESH,
        )
        down = pltpu.make_async_remote_copy(
            src_ref=ref.at[:, pl.ds(WIDE, WIDE), pl.ds(0, span)],
            dst_ref=ref.at[:, pl.ds(WIDE + rows, WIDE), pl.ds(0, span)],
            send_sem=row_send.at[2 * number + 1], recv_sem=row_recv.at[2 * number + 1],
            device_id={"lat": south}, device_id_type=MESH,
        )
        up.start()
        down.start()
        up.wait()
        down.wait()
        lane = lax.broadcasted_iota(jnp.int32, (high, LANES), 1)
        last = (cols - WIDE) // LANES * LANES
        inset = cols - WIDE - last
        eastern = western = None
        for f in range(fields):
            e = pltpu.roll(ref[f, :, last : last + LANES], (WIDE * f - inset) % LANES, 1)
            w = pltpu.roll(ref[f, :, :LANES], WIDE * f, 1) if f else ref[f, :, :LANES]
            eastern = jnp.where(lane >= WIDE * f, e, eastern) if f else e
            western = jnp.where(lane >= WIDE * f, w, western) if f else w
        east_out[number] = eastern
        west_out[number] = western
        right = pltpu.make_async_remote_copy(
            src_ref=east_out.at[number], dst_ref=west_in.at[number],
            send_sem=col_send.at[2 * number], recv_sem=col_recv.at[2 * number],
            device_id={"lon": east}, device_id_type=MESH,
        )
        left = pltpu.make_async_remote_copy(
            src_ref=west_out.at[number], dst_ref=east_in.at[number],
            send_sem=col_send.at[2 * number + 1], recv_sem=col_recv.at[2 * number + 1],
            device_id={"lon": west}, device_id_type=MESH,
        )
        right.start()
        left.start()
        right.wait()
        left.wait()
        start = wid - LANES
        own = cols - start
        from_east, from_west = east_in[number], west_in[number]
        for f, fill in enumerate(fills):
            e = pltpu.roll(from_east, (own - WIDE * f) % LANES, 1)
            w = pltpu.roll(from_west, (LANES - WIDE - WIDE * f) % LANES, 1)
            halo = jnp.where(lane < own + WIDE, e, jnp.where(lane >= LANES - WIDE, w, fill))
            if own:
                halo = jnp.where(lane < own, ref[f, :, start:], halo)
            ref[f, :, start:] = halo

    exchange(x_ref, 0, (1.0,) + (0.0,) * 7)

    def below(ref, f, r):
        if r == 0:
            return pltpu.roll(ref[f, :block, :], 1, 0)
        return pltpu.roll(ref[f, r - TILE : r + block, :], 1, 0)[TILE:]

    for r in range(0, high, block):
        here = pl.ds(r, block)
        d, m, g = x_ref[0, here, :], x_ref[1, here, :], x_ref[2, here, :]
        for side, shifted in enumerate(
            (lambda f, v: pltpu.roll(v, 1, 1), lambda f, v: below(x_ref, f, r))
        ):
            both = d + shifted(0, d)
            wet = m * shifted(1, m)
            st_ref[side, here, :] = wet * (1.0 - (g + shifted(2, g)) / both)
            st_ref[2 + side, here, :] = 0.7 * wet
            st_ref[4 + side, here, :] = 0.3 * both
        st_ref[6, here, :] = m
        st_ref[7, here, :] = m * x_ref[3, here, :]
        st_ref[8, here, :] = m * x_ref[4, here, :]
    gain_ref[0] = x_ref[1, mine, :span]
    for side in range(2):
        g = st_ref[side, mine, :span]
        for _ in range(STEPS.bit_length() - 1):
            g = g * g
        gain_ref[1 + side] = g
    acc_ref[...] = jnp.zeros(acc_ref.shape, jnp.float32)

    def sweep(ref, base, want):
        def step(t, nothing):
            cosine = trig_ref[2 * (k * STEPS + t)]
            sine = trig_ref[2 * (k * STEPS + t) + 1]
            carry = None
            for r in reversed(range(0, high, block)):
                here = pl.ds(r, block)
                a = ref[base, here, :]
                p = st_ref[0, here, :] * ref[base + 1, here, :] - st_ref[2, here, :] * (
                    a - pltpu.roll(a, 1, 1)
                )
                q = st_ref[1, here, :] * ref[base + 2, here, :] - st_ref[3, here, :] * (
                    a - below(ref, base, r)
                )
                u = st_ref[4, here, :] * p
                v = st_ref[5, here, :] * q
                if carry is None:
                    v_north = pltpu.roll(v, block - 1, 0)
                else:
                    v_north = pltpu.roll(
                        jnp.concatenate([v, carry], axis=0), block + TILE - 1, 0
                    )[:block]
                carry = v[:TILE]
                spread = (pltpu.roll(u, wid - 1, 1) - u) + (v_north - v)
                ref[base, here, :] = st_ref[6, here, :] * (a - spread) + (
                    st_ref[7, here, :] * cosine + st_ref[8, here, :] * sine
                )
                ref[base + 1, here, :] = p
                ref[base + 2, here, :] = q
                if want:
                    low, top = max(r, WIDE), min(r + block, WIDE + rows + TILE)
                    part = pl.ds(low, top - low)
                    p, q = p[low - r : top - r], q[low - r : top - r]
                    acc_ref[0, part, :] += cosine * p
                    acc_ref[1, part, :] += sine * p
                    acc_ref[2, part, :] += cosine * q
                    acc_ref[3, part, :] += sine * q
            return nothing

        lax.fori_loop(0, STEPS, step, 0)

    half = n // 2
    place = jnp.where(k < half, k, n - 1 - k)
    inner, outer = jnp.where(k < half, later, sooner), jnp.where(k < half, sooner, later)

    def gather():
        return pltpu.make_async_remote_copy(
            src_ref=term_ref, dst_ref=part_ref, send_sem=t_send.at[0], recv_sem=t_recv.at[0],
            device_id={"tm": inner}, device_id_type=MESH,
        )

    def swap():
        return pltpu.make_async_remote_copy(
            src_ref=term_ref, dst_ref=other_ref, send_sem=t_send.at[1], recv_sem=t_recv.at[1],
            device_id={"tm": inner}, device_id_type=MESH,
        )

    def spread_out():
        return pltpu.make_async_remote_copy(
            src_ref=tot_ref, dst_ref=tot_ref, send_sem=t_send.at[2], recv_sem=t_recv.at[2],
            device_id={"tm": outer}, device_id_type=MESH,
        )

    def inward():
        @pl.when(place > 0)
        def _():
            gather().wait_recv()
            term_ref[...] += part_ref[...]

        @pl.when(place < half - 1)
        def _():
            gather().start()

        @pl.when(place == half - 1)
        def _():
            swap().start()

    def outward():
        @pl.when(place == half - 1)
        def _():
            swap().wait_recv()
            tot_ref[...] = term_ref[...] + other_ref[...]

        @pl.when(place < half - 1)
        def _():
            spread_out().wait_recv()

        @pl.when(place > 0)
        def _():
            spread_out().start()

    def settle():
        @pl.when(place < half - 1)
        def _():
            gather().wait_send()

        @pl.when(place == half - 1)
        def _():
            swap().wait_send()

        @pl.when(place > 0)
        def _():
            spread_out().wait_send()

    def relay(ref, base, number, c_ref, cs_ref, e_ref, want):
        def piece(chunk):
            return pl.ds(pl.multiple_of(chunk * TILE, TILE), TILE)

        def forward(chunk):
            return pltpu.make_async_remote_copy(
                src_ref=cs_ref.at[:, piece(chunk)], dst_ref=c_ref.at[:, piece(chunk)],
                send_sem=c_send.at[number, chunk], recv_sem=c_recv.at[number, chunk],
                device_id={"tm": later}, device_id_type=MESH,
            )

        def back(chunk):
            return pltpu.make_async_remote_copy(
                src_ref=e_ref.at[:, piece(chunk)], dst_ref=e_ref.at[:, piece(chunk)],
                send_sem=e_send.at[number, chunk], recv_sem=e_recv.at[number, chunk],
                device_id={"tm": sooner}, device_id_type=MESH,
            )

        @pl.when(k == 0)
        def _():
            c_ref[...] = jnp.zeros(c_ref.shape, jnp.float32)

        @pl.when(k == n - 1)
        def _():
            for f in range(3):
                e_ref[f] = ref[base + f, mine, :span]

        turns = count + SKEW * (n - 1)

        def turn(i, nothing):
            if want:
                pl.when(i == 8 * place)(inward)
                pl.when(i == jnp.minimum(8 * (n - 1 - place), turns - 1))(outward)

            ahead = i - SKEW * k

            @pl.when((ahead >= 0) & (ahead < count))
            def _():
                @pl.when(k > 0)
                def _():
                    forward(ahead).wait_recv()

                here = piece(ahead)
                there = pl.ds(pl.multiple_of(WIDE + ahead * TILE, TILE), TILE)

                @pl.when(k < n - 1)
                def _():
                    for f in range(3):
                        cs_ref[f, here, :] = ref[base + f, there, :span] + gain_ref[f, here, :] * (
                            c_ref[f, here, :] - old_ref[f, here, :]
                        )
                    forward(ahead).start()

            behind = i - SKEW * (n - 1 - k)

            @pl.when((behind >= 0) & (behind < count))
            def _():
                @pl.when(k < n - 1)
                def _():
                    back(behind).wait_recv()

                @pl.when(k > 0)
                def _():
                    back(behind).start()

            return nothing

        lax.fori_loop(0, turns, turn, 0)

        for f in range(3):
            power = e_ref[f]
            for j in range(n - 1):
                power = power * jnp.where(j < k, gain_ref[f], 1.0)
            fresh = c_ref[f] + power
            if want:
                out_ref[0, f] = fresh[:, :cols]
            else:
                old_ref[f] = fresh
                y_ref[f, mine, :span] = fresh

        def sent(chunk, nothing):
            @pl.when(k < n - 1)
            def _():
                forward(chunk).wait_send()

            @pl.when(k > 0)
            def _():
                back(chunk).wait_send()

            return nothing

        return lambda: lax.fori_loop(0, count, sent, 0)

    for f in range(3):
        old_ref[f] = x_ref[5 + f, mine, :span]
    sweep(x_ref, 5, False)
    finish_first = relay(x_ref, 5, 0, c1_ref, cs1_ref, e1_ref, False)
    exchange(y_ref, 1, (0.0,) * 3)
    sweep(y_ref, 0, True)

    loads[7].wait()
    weight = 0.5 * x_ref[1, mine, :span] / x_ref[0, mine, :span]
    term = jnp.zeros((rows, span), jnp.float32)
    for f in range(4):
        if f < 2:
            v = acc_ref[f, mine, :]
            mid = (v + pltpu.roll(v, wid - 1, 1))[:, :span]
        else:
            v = acc_ref[f, pl.ds(WIDE, rows + TILE), :span]
            mid = (v + pltpu.roll(v, rows + TILE - 1, 0))[:rows]
        flow = flow_ref[f]
        if span > cols:
            flow = jnp.concatenate([flow, jnp.zeros((rows, span - cols), jnp.float32)], axis=1)
        term = term + flow * mid
    term_ref[...] = weight * term

    finish_second = relay(y_ref, 0, 1, c2_ref, cs2_ref, e2_ref, True)
    grad_ref[...] = tot_ref[:, :cols] * (1.0 / (n * STEPS))
    settle()
    finish_first()
    finish_second()


def shards(
    sizes, depth_class, ocean_mask, depth_levels, drag, tide_force, forward_flow, guess
):
    n = sizes[0]
    rows, cols = ocean_mask.shape
    high = rows + 2 * WIDE
    wid = -(-(cols + 2 * WIDE) // LANES) * LANES
    span = -(-cols // LANES) * LANES
    count = rows // TILE
    assert n % 2 == 0 and rows % TILE == 0 and rows >= WIDE and wid - LANES <= cols
    counts = np.arange(1, n * STEPS + 1)
    angle = 2.0 * math.pi * counts / (n * STEPS)
    trig = jnp.asarray(np.stack([np.cos(angle), np.sin(angle)], axis=1).reshape(-1), jnp.float32)
    f32 = jnp.float32
    vmem = pl.BlockSpec(memory_space=pltpu.VMEM)
    dma = pltpu.SemaphoreType.DMA
    return pl.pallas_call(
        functools.partial(kernel, sizes),
        out_shape=(
            jax.ShapeDtypeStruct((1, 3, rows, cols), f32),
            jax.ShapeDtypeStruct((rows, cols), f32),
        ),
        in_specs=[pl.BlockSpec(memory_space=pl.ANY)] * 8,
        out_specs=(vmem, vmem),
        scratch_shapes=[
            pltpu.VMEM((rows, cols), jnp.int32),
            pltpu.VMEM((rows, cols), jnp.int32),
            pltpu.SMEM(depth_levels.shape, f32),
            pltpu.VMEM((rows, cols), f32),
            pltpu.VMEM(tide_force.shape, f32),
            pltpu.VMEM(forward_flow.shape, f32),
            pltpu.VMEM(guess.shape, f32),
            pltpu.SMEM(trig.shape, f32),
            dma((8,)),
            pltpu.VMEM((8, high, wid), f32),
            pltpu.VMEM((3, high, wid), f32),
            pltpu.VMEM((9, high, wid), f32),
            pltpu.VMEM((4, high, wid), f32),
            pltpu.VMEM((3, rows, span), f32),
            pltpu.VMEM((3, rows, span), f32),
            pltpu.VMEM((rows, span), f32),
            pltpu.VMEM((2, high, LANES), f32),
            pltpu.VMEM((2, high, LANES), f32),
            pltpu.VMEM((2, high, LANES), f32),
            pltpu.VMEM((2, high, LANES), f32),
            pltpu.VMEM((3, rows, span), f32),
            pltpu.VMEM((3, rows, span), f32),
            pltpu.VMEM((3, rows, span), f32),
            pltpu.VMEM((3, rows, span), f32),
            pltpu.VMEM((3, rows, span), f32),
            pltpu.VMEM((3, rows, span), f32),
            pltpu.VMEM((rows, span), f32),
            pltpu.VMEM((rows, span), f32),
            pltpu.VMEM((rows, span), f32),
            dma((4,)), dma((4,)), dma((4,)), dma((4,)),
            dma((2, count)), dma((2, count)), dma((2, count)), dma((2, count)),
            dma((3,)), dma((3,)),
        ],
        compiler_params=pltpu.CompilerParams(
            collective_id=0, has_side_effects=True, vmem_limit_bytes=56 * 1024 * 1024
        ),
        name="parareal",
    )(depth_class, ocean_mask, depth_levels, drag, tide_force, forward_flow, guess, trig)


def solution(mesh):
    sizes = tuple(mesh.shape[axis] for axis in ("tm", "lat", "lon"))
    return jax.shard_map(
        functools.partial(shards, sizes),
        mesh=mesh,
        in_specs=(
            P("lat", "lon"),
            P("lat", "lon"),
            P(),
            P("lat", "lon"),
            P(None, "lat", "lon"),
            P(None, "lat", "lon"),
            P("tm", None, "lat", "lon"),
        ),
        out_specs=(P("tm", None, "lat", "lon"), P("lat", "lon")),
        check_vma=False,
    )
```

```python
import functools
import math

import jax
import jax.numpy as jnp
import numpy as np
from jax import lax
from jax.experimental import pallas as pl
from jax.experimental.pallas import tpu as pltpu
from jax.sharding import PartitionSpec as P

STEPS = 16
SWEEPS = 2
DCLASS = 32
WIDE = STEPS
LANES = 128
TILE = 8
SKEW = 5

MESH = pl.DeviceIdType.MESH


def kernel(
    sizes, cls_hbm, ocean_hbm, lev_hbm, drag_hbm, force_hbm, flow_hbm, guess_hbm, trig_hbm,
    out_ref, grad_ref,
    cls_ref, ocean_ref, lev_ref, drag_ref, force_ref, flow_ref, guess_ref, trig_ref, load_sem,
    x_ref, y_ref, st_ref, acc_ref, gain_ref, old_ref, term_ref, east_out, west_out, east_in, west_in,
    c1_ref, cs1_ref, e1_ref, c2_ref, cs2_ref, e2_ref, part_ref, other_ref, tot_ref,
    row_send, row_recv, col_send, col_recv,
    c_send, c_recv, e_send, e_recv, t_send, t_recv,
):
    n, n_lat, n_lon = sizes
    rows, cols = ocean_ref.shape
    high, wid = x_ref.shape[1], x_ref.shape[2]
    span = c1_ref.shape[2]
    block = TILE * max(d for d in (1, 2, 3) if (high // TILE) % d == 0)
    count = rows // TILE
    k, lat, lon = lax.axis_index("tm"), lax.axis_index("lat"), lax.axis_index("lon")
    north, south = lax.rem(lat + 1, n_lat), lax.rem(lat + n_lat - 1, n_lat)
    east, west = lax.rem(lon + 1, n_lon), lax.rem(lon + n_lon - 1, n_lon)
    later, sooner = lax.rem(k + 1, n), lax.rem(k + n - 1, n)

    loads = [
        pltpu.make_async_copy(source, target, load_sem.at[i])
        for i, (source, target) in enumerate((
            (lev_hbm, lev_ref), (cls_hbm, cls_ref), (ocean_hbm, ocean_ref), (drag_hbm, drag_ref),
            (force_hbm, force_ref), (guess_hbm, guess_ref), (trig_hbm, trig_ref), (flow_hbm, flow_ref),
        ))
    ]
    for load in loads:
        load.start()
    barrier = pltpu.get_barrier_semaphore()
    for axis, spot in (
        ("lat", north), ("lat", south), ("lon", east), ("lon", west), ("tm", later), ("tm", sooner)
    ):
        pl.semaphore_signal(barrier, inc=1, device_id={axis: spot}, device_id_type=MESH)
    for y in (north, south):
        for x in (east, west):
            pl.semaphore_signal(barrier, inc=1, device_id={"lat": y, "lon": x}, device_id_type=MESH)

    mine = pl.ds(WIDE, rows)
    loads[0].wait()
    loads[1].wait()
    classes = cls_ref[...]
    depth = jnp.zeros((rows, cols), jnp.float32)
    for c in range(DCLASS):
        depth = jnp.where(classes == c, lev_ref[c], depth)
    x_ref[0, mine, :cols] = depth
    for load in loads[2:7]:
        load.wait()
    line = lat * rows + lax.broadcasted_iota(jnp.int32, (rows, cols), 0)
    polar = (line == 0) | (line == n_lat * rows - 1)
    x_ref[1, mine, :cols] = jnp.where(polar, 0, ocean_ref[...]).astype(jnp.float32)
    x_ref[2, mine, :cols] = drag_ref[...]
    for f in range(2):
        x_ref[3 + f, mine, :cols] = force_ref[f]
    for f in range(3):
        x_ref[5 + f, mine, :cols] = guess_ref[0, f]
    pl.semaphore_wait(barrier, 10)

    def exchange(ref, number, fills):
        fields = len(fills)
        up = pltpu.make_async_remote_copy(
            src_ref=ref.at[:, pl.ds(rows, WIDE), pl.ds(0, span)],
            dst_ref=ref.at[:, pl.ds(0, WIDE), pl.ds(0, span)],
            send_sem=row_send.at[2 * number], recv_sem=row_recv.at[2 * number],
            device_id={"lat": north}, device_id_type=MESH,
        )
        down = pltpu.make_async_remote_copy(
            src_ref=ref.at[:, pl.ds(WIDE, WIDE), pl.ds(0, span)],
            dst_ref=ref.at[:, pl.ds(WIDE + rows, WIDE), pl.ds(0, span)],
            send_sem=row_send.at[2 * number + 1], recv_sem=row_recv.at[2 * number + 1],
            device_id={"lat": south}, device_id_type=MESH,
        )
        up.start()
        down.start()
        small = lax.broadcasted_iota(jnp.int32, (rows, LANES), 1)
        last = (cols - WIDE) // LANES * LANES
        inset = cols - WIDE - last
        eastern = western = None
        for f in range(fields):
            e = pltpu.roll(ref[f, mine, last : last + LANES], (WIDE * f - inset) % LANES, 1)
            w = ref[f, mine, :LANES]
            w = pltpu.roll(w, WIDE * f, 1) if f else w
            eastern = jnp.where(small >= WIDE * f, e, eastern) if f else e
            western = jnp.where(small >= WIDE * f, w, western) if f else w
        east_out[number] = eastern
        west_out[number] = western
        copies = [up, down]
        for side, (x, source, target) in enumerate(((east, east_out, west_in), (west, west_out, east_in))):
            for y, first, extent, landing in (
                (None, 0, rows, WIDE), (north, rows - WIDE, WIDE, 0), (south, 0, WIDE, WIDE + rows)
            ):
                slot = 6 * number + len(copies) - 2
                copies.append(
                    pltpu.make_async_remote_copy(
                        src_ref=source.at[number, pl.ds(first, extent)],
                        dst_ref=target.at[number, pl.ds(landing, extent)],
                        send_sem=col_send.at[slot], recv_sem=col_recv.at[slot],
                        device_id={"lon": x} if y is None else {"lat": y, "lon": x},
                        device_id_type=MESH,
                    )
                )
                copies[-1].start()
        for copy in copies:
            copy.wait()
        lane = lax.broadcasted_iota(jnp.int32, (high, LANES), 1)
        start = wid - LANES
        own = cols - start
        from_east, from_west = east_in[number], west_in[number]
        for f, fill in enumerate(fills):
            e = pltpu.roll(from_east, (own - WIDE * f) % LANES, 1)
            w = pltpu.roll(from_west, (LANES - WIDE - WIDE * f) % LANES, 1)
            halo = jnp.where(lane < own + WIDE, e, jnp.where(lane >= LANES - WIDE, w, fill))
            if own:
                halo = jnp.where(lane < own, ref[f, :, start:], halo)
            ref[f, :, start:] = halo

    exchange(x_ref, 0, (1.0,) + (0.0,) * 7)

    def below(ref, f, r):
        if r == 0:
            return pltpu.roll(ref[f, :block, :], 1, 0)
        return pltpu.roll(ref[f, r - TILE : r + block, :], 1, 0)[TILE:]

    for r in range(0, high, block):
        here = pl.ds(r, block)
        d, m, g = x_ref[0, here, :], x_ref[1, here, :], x_ref[2, here, :]
        for side, shifted in enumerate(
            (lambda f, v: pltpu.roll(v, 1, 1), lambda f, v: below(x_ref, f, r))
        ):
            both = d + shifted(0, d)
            wet = m * shifted(1, m)
            st_ref[side, here, :] = wet * (1.0 - (g + shifted(2, g)) / both)
            st_ref[2 + side, here, :] = 0.7 * wet
            st_ref[4 + side, here, :] = 0.3 * both
        st_ref[6, here, :] = m
        st_ref[7, here, :] = m * x_ref[3, here, :]
        st_ref[8, here, :] = m * x_ref[4, here, :]
    gain_ref[0] = x_ref[1, mine, :span]
    for side in range(2):
        g = st_ref[side, mine, :span]
        for _ in range(STEPS.bit_length() - 1):
            g = g * g
        gain_ref[1 + side] = g
    acc_ref[...] = jnp.zeros(acc_ref.shape, jnp.float32)

    def sweep(ref, base, want):
        def step(t, nothing):
            cosine = trig_ref[2 * (k * STEPS + t)]
            sine = trig_ref[2 * (k * STEPS + t) + 1]
            carry = None
            for r in reversed(range(0, high, block)):
                here = pl.ds(r, block)
                a = ref[base, here, :]
                p = st_ref[0, here, :] * ref[base + 1, here, :] - st_ref[2, here, :] * (
                    a - pltpu.roll(a, 1, 1)
                )
                q = st_ref[1, here, :] * ref[base + 2, here, :] - st_ref[3, here, :] * (
                    a - below(ref, base, r)
                )
                u = st_ref[4, here, :] * p
                v = st_ref[5, here, :] * q
                if carry is None:
                    v_north = pltpu.roll(v, block - 1, 0)
                else:
                    v_north = pltpu.roll(
                        jnp.concatenate([v, carry], axis=0), block + TILE - 1, 0
                    )[:block]
                carry = v[:TILE]
                spread = (pltpu.roll(u, wid - 1, 1) - u) + (v_north - v)
                ref[base, here, :] = st_ref[6, here, :] * (a - spread) + (
                    st_ref[7, here, :] * cosine + st_ref[8, here, :] * sine
                )
                ref[base + 1, here, :] = p
                ref[base + 2, here, :] = q
                if want:
                    low, top = max(r, WIDE), min(r + block, WIDE + rows + TILE)
                    part = pl.ds(low, top - low)
                    p, q = p[low - r : top - r], q[low - r : top - r]
                    acc_ref[0, part, :] += cosine * p
                    acc_ref[1, part, :] += sine * p
                    acc_ref[2, part, :] += cosine * q
                    acc_ref[3, part, :] += sine * q
            return nothing

        lax.fori_loop(0, STEPS, step, 0)

    half = n // 2
    place = jnp.where(k < half, k, n - 1 - k)
    inner, outer = jnp.where(k < half, later, sooner), jnp.where(k < half, sooner, later)

    def gather():
        return pltpu.make_async_remote_copy(
            src_ref=term_ref, dst_ref=part_ref, send_sem=t_send.at[0], recv_sem=t_recv.at[0],
            device_id={"tm": inner}, device_id_type=MESH,
        )

    def swap():
        return pltpu.make_async_remote_copy(
            src_ref=term_ref, dst_ref=other_ref, send_sem=t_send.at[1], recv_sem=t_recv.at[1],
            device_id={"tm": inner}, device_id_type=MESH,
        )

    def spread_out():
        return pltpu.make_async_remote_copy(
            src_ref=tot_ref, dst_ref=tot_ref, send_sem=t_send.at[2], recv_sem=t_recv.at[2],
            device_id={"tm": outer}, device_id_type=MESH,
        )

    def inward():
        @pl.when(place > 0)
        def _():
            gather().wait_recv()
            term_ref[...] += part_ref[...]

        @pl.when(place < half - 1)
        def _():
            gather().start()

        @pl.when(place == half - 1)
        def _():
            swap().start()

    def outward():
        @pl.when(place == half - 1)
        def _():
            swap().wait_recv()
            tot_ref[...] = term_ref[...] + other_ref[...]

        @pl.when(place < half - 1)
        def _():
            spread_out().wait_recv()

        @pl.when(place > 0)
        def _():
            spread_out().start()

    def settle():
        @pl.when(place < half - 1)
        def _():
            gather().wait_send()

        @pl.when(place == half - 1)
        def _():
            swap().wait_send()

        @pl.when(place > 0)
        def _():
            spread_out().wait_send()

    def relay(ref, base, number, c_ref, cs_ref, e_ref, want):
        def piece(chunk):
            return pl.ds(pl.multiple_of(chunk * TILE, TILE), TILE)

        def forward(chunk):
            return pltpu.make_async_remote_copy(
                src_ref=cs_ref.at[:, piece(chunk)], dst_ref=c_ref.at[:, piece(chunk)],
                send_sem=c_send.at[number, chunk], recv_sem=c_recv.at[number, chunk],
                device_id={"tm": later}, device_id_type=MESH,
            )

        def back(chunk):
            return pltpu.make_async_remote_copy(
                src_ref=e_ref.at[:, piece(chunk)], dst_ref=e_ref.at[:, piece(chunk)],
                send_sem=e_send.at[number, chunk], recv_sem=e_recv.at[number, chunk],
                device_id={"tm": sooner}, device_id_type=MESH,
            )

        @pl.when(k == 0)
        def _():
            c_ref[...] = jnp.zeros(c_ref.shape, jnp.float32)

        @pl.when(k == n - 1)
        def _():
            for f in range(3):
                e_ref[f] = ref[base + f, mine, :span]

        turns = count + SKEW * (n - 1)

        def turn(i, nothing):
            if want:
                pl.when(i == 8 * place)(inward)
                pl.when(i == jnp.minimum(8 * (n - 1 - place), turns - 1))(outward)

            ahead = i - SKEW * k

            @pl.when((ahead >= 0) & (ahead < count))
            def _():
                @pl.when(k > 0)
                def _():
                    forward(ahead).wait_recv()

                here = piece(ahead)
                there = pl.ds(pl.multiple_of(WIDE + ahead * TILE, TILE), TILE)

                @pl.when(k < n - 1)
                def _():
                    for f in range(3):
                        cs_ref[f, here, :] = ref[base + f, there, :span] + gain_ref[f, here, :] * (
                            c_ref[f, here, :] - old_ref[f, here, :]
                        )
                    forward(ahead).start()

            behind = i - SKEW * (n - 1 - k)

            @pl.when((behind >= 0) & (behind < count))
            def _():
                @pl.when(k < n - 1)
                def _():
                    back(behind).wait_recv()

                @pl.when(k > 0)
                def _():
                    back(behind).start()

            return nothing

        lax.fori_loop(0, turns, turn, 0)

        for f in range(3):
            power = e_ref[f]
            for j in range(n - 1):
                power = power * jnp.where(j < k, gain_ref[f], 1.0)
            fresh = c_ref[f] + power
            if want:
                out_ref[0, f] = fresh[:, :cols]
            else:
                old_ref[f] = fresh
                y_ref[f, mine, :span] = fresh

        def sent(chunk, nothing):
            @pl.when(k < n - 1)
            def _():
                forward(chunk).wait_send()

            @pl.when(k > 0)
            def _():
                back(chunk).wait_send()

            return nothing

        return lambda: lax.fori_loop(0, count, sent, 0)

    for f in range(3):
        old_ref[f] = x_ref[5 + f, mine, :span]
    sweep(x_ref, 5, False)
    finish_first = relay(x_ref, 5, 0, c1_ref, cs1_ref, e1_ref, False)
    exchange(y_ref, 1, (0.0,) * 3)
    sweep(y_ref, 0, True)

    loads[7].wait()
    weight = 0.5 * x_ref[1, mine, :span] / x_ref[0, mine, :span]
    term = jnp.zeros((rows, span), jnp.float32)
    for f in range(4):
        if f < 2:
            v = acc_ref[f, mine, :]
            mid = (v + pltpu.roll(v, wid - 1, 1))[:, :span]
        else:
            v = acc_ref[f, pl.ds(WIDE, rows + TILE), :span]
            mid = (v + pltpu.roll(v, rows + TILE - 1, 0))[:rows]
        flow = flow_ref[f]
        if span > cols:
            flow = jnp.concatenate([flow, jnp.zeros((rows, span - cols), jnp.float32)], axis=1)
        term = term + flow * mid
    term_ref[...] = weight * term

    finish_second = relay(y_ref, 0, 1, c2_ref, cs2_ref, e2_ref, True)
    grad_ref[...] = tot_ref[:, :cols] * (1.0 / (n * STEPS))
    settle()
    finish_first()
    finish_second()


def shards(
    sizes, depth_class, ocean_mask, depth_levels, drag, tide_force, forward_flow, guess
):
    n = sizes[0]
    rows, cols = ocean_mask.shape
    high = rows + 2 * WIDE
    wid = -(-(cols + 2 * WIDE) // LANES) * LANES
    span = -(-cols // LANES) * LANES
    count = rows // TILE
    assert n % 2 == 0 and rows % TILE == 0 and rows >= WIDE and wid - LANES <= cols
    counts = np.arange(1, n * STEPS + 1)
    angle = 2.0 * math.pi * counts / (n * STEPS)
    trig = jnp.asarray(np.stack([np.cos(angle), np.sin(angle)], axis=1).reshape(-1), jnp.float32)
    f32 = jnp.float32
    vmem = pl.BlockSpec(memory_space=pltpu.VMEM)
    dma = pltpu.SemaphoreType.DMA
    return pl.pallas_call(
        functools.partial(kernel, sizes),
        out_shape=(
            jax.ShapeDtypeStruct((1, 3, rows, cols), f32),
            jax.ShapeDtypeStruct((rows, cols), f32),
        ),
        in_specs=[pl.BlockSpec(memory_space=pl.ANY)] * 8,
        out_specs=(vmem, vmem),
        scratch_shapes=[
            pltpu.VMEM((rows, cols), jnp.int32),
            pltpu.VMEM((rows, cols), jnp.int32),
            pltpu.SMEM(depth_levels.shape, f32),
            pltpu.VMEM((rows, cols), f32),
            pltpu.VMEM(tide_force.shape, f32),
            pltpu.VMEM(forward_flow.shape, f32),
            pltpu.VMEM(guess.shape, f32),
            pltpu.SMEM(trig.shape, f32),
            dma((8,)),
            pltpu.VMEM((8, high, wid), f32),
            pltpu.VMEM((3, high, wid), f32),
            pltpu.VMEM((9, high, wid), f32),
            pltpu.VMEM((4, high, wid), f32),
            pltpu.VMEM((3, rows, span), f32),
            pltpu.VMEM((3, rows, span), f32),
            pltpu.VMEM((rows, span), f32),
            pltpu.VMEM((2, rows, LANES), f32),
            pltpu.VMEM((2, rows, LANES), f32),
            pltpu.VMEM((2, high, LANES), f32),
            pltpu.VMEM((2, high, LANES), f32),
            pltpu.VMEM((3, rows, span), f32),
            pltpu.VMEM((3, rows, span), f32),
            pltpu.VMEM((3, rows, span), f32),
            pltpu.VMEM((3, rows, span), f32),
            pltpu.VMEM((3, rows, span), f32),
            pltpu.VMEM((3, rows, span), f32),
            pltpu.VMEM((rows, span), f32),
            pltpu.VMEM((rows, span), f32),
            pltpu.VMEM((rows, span), f32),
            dma((4,)), dma((4,)), dma((12,)), dma((12,)),
            dma((2, count)), dma((2, count)), dma((2, count)), dma((2, count)),
            dma((3,)), dma((3,)),
        ],
        compiler_params=pltpu.CompilerParams(
            collective_id=0, has_side_effects=True, vmem_limit_bytes=56 * 1024 * 1024
        ),
        name="parareal",
    )(depth_class, ocean_mask, depth_levels, drag, tide_force, forward_flow, guess, trig)


def solution(mesh):
    sizes = tuple(mesh.shape[axis] for axis in ("tm", "lat", "lon"))
    return jax.shard_map(
        functools.partial(shards, sizes),
        mesh=mesh,
        in_specs=(
            P("lat", "lon"),
            P("lat", "lon"),
            P(),
            P("lat", "lon"),
            P(None, "lat", "lon"),
            P(None, "lat", "lon"),
            P("tm", None, "lat", "lon"),
        ),
        out_specs=(P("tm", None, "lat", "lon"), P("lat", "lon")),
        check_vma=False,
    )
```

```python
import functools
import math

import jax
import jax.numpy as jnp
import numpy as np
from jax import lax
from jax.experimental import pallas as pl
from jax.experimental.pallas import tpu as pltpu
from jax.sharding import PartitionSpec as P

STEPS = 16
SWEEPS = 2
DCLASS = 32
WIDE = STEPS
LANES = 128
TILE = 8
EARLY = 8
SKEW = 5

MESH = pl.DeviceIdType.MESH


def kernel(
    sizes, cls_hbm, ocean_hbm, lev_hbm, drag_hbm, force_hbm, flow_hbm, guess_hbm, trig_hbm,
    out_ref, grad_ref,
    cls_ref, ocean_ref, lev_ref, drag_ref, force_ref, flow_ref, guess_ref, trig_ref, load_sem,
    x_ref, y_ref, b_ref, end_ref, st_ref, acc_ref, gain_ref, old_ref, term_ref, east_out, west_out, east_in, west_in,
    c1_ref, cs1_ref, e1_ref, c2_ref, cs2_ref, e2_ref, part_ref, other_ref, tot_ref,
    row_send, row_recv, col_send, col_recv,
    c_send, c_recv, e_send, e_recv, t_send, t_recv,
):
    n, n_lat, n_lon = sizes
    rows, cols = ocean_ref.shape
    high, wid = x_ref.shape[1], x_ref.shape[2]
    span = c1_ref.shape[2]
    block = 2 * TILE
    cut = EARLY * TILE
    count = rows // TILE
    k, lat, lon = lax.axis_index("tm"), lax.axis_index("lat"), lax.axis_index("lon")
    north, south = lax.rem(lat + 1, n_lat), lax.rem(lat + n_lat - 1, n_lat)
    east, west = lax.rem(lon + 1, n_lon), lax.rem(lon + n_lon - 1, n_lon)
    later, sooner = lax.rem(k + 1, n), lax.rem(k + n - 1, n)

    loads = [
        pltpu.make_async_copy(source, target, load_sem.at[i])
        for i, (source, target) in enumerate((
            (lev_hbm, lev_ref), (cls_hbm, cls_ref), (ocean_hbm, ocean_ref), (drag_hbm, drag_ref),
            (force_hbm, force_ref), (guess_hbm, guess_ref), (trig_hbm, trig_ref), (flow_hbm, flow_ref),
        ))
    ]
    for load in loads:
        load.start()
    barrier = pltpu.get_barrier_semaphore()
    for axis, spot in (
        ("lat", north), ("lat", south), ("lon", east), ("lon", west), ("tm", later), ("tm", sooner)
    ):
        pl.semaphore_signal(barrier, inc=1, device_id={axis: spot}, device_id_type=MESH)
    for y in (north, south):
        for x in (east, west):
            pl.semaphore_signal(barrier, inc=1, device_id={"lat": y, "lon": x}, device_id_type=MESH)

    mine = pl.ds(WIDE, rows)
    loads[0].wait()
    loads[1].wait()
    classes = cls_ref[...]
    depth = jnp.zeros((rows, cols), jnp.float32)
    for c in range(DCLASS):
        depth = jnp.where(classes == c, lev_ref[c], depth)
    x_ref[0, mine, :cols] = depth
    for load in loads[2:7]:
        load.wait()
    line = lat * rows + lax.broadcasted_iota(jnp.int32, (rows, cols), 0)
    polar = (line == 0) | (line == n_lat * rows - 1)
    x_ref[1, mine, :cols] = jnp.where(polar, 0, ocean_ref[...]).astype(jnp.float32)
    x_ref[2, mine, :cols] = drag_ref[...]
    for f in range(2):
        x_ref[3 + f, mine, :cols] = force_ref[f]
    for f in range(3):
        x_ref[5 + f, mine, :cols] = guess_ref[0, f]
    pl.semaphore_wait(barrier, 10)

    def exchange(ref, number, fills):
        fields = len(fills)
        up = pltpu.make_async_remote_copy(
            src_ref=ref.at[:, pl.ds(rows, WIDE), pl.ds(0, span)],
            dst_ref=ref.at[:, pl.ds(0, WIDE), pl.ds(0, span)],
            send_sem=row_send.at[2 * number], recv_sem=row_recv.at[2 * number],
            device_id={"lat": north}, device_id_type=MESH,
        )
        down = pltpu.make_async_remote_copy(
            src_ref=ref.at[:, pl.ds(WIDE, WIDE), pl.ds(0, span)],
            dst_ref=ref.at[:, pl.ds(WIDE + rows, WIDE), pl.ds(0, span)],
            send_sem=row_send.at[2 * number + 1], recv_sem=row_recv.at[2 * number + 1],
            device_id={"lat": south}, device_id_type=MESH,
        )
        up.start()
        down.start()
        small = lax.broadcasted_iota(jnp.int32, (rows, LANES), 1)
        last = (cols - WIDE) // LANES * LANES
        inset = cols - WIDE - last
        eastern = western = None
        for f in range(fields):
            e = pltpu.roll(ref[f, mine, last : last + LANES], (WIDE * f - inset) % LANES, 1)
            w = ref[f, mine, :LANES]
            w = pltpu.roll(w, WIDE * f, 1) if f else w
            eastern = jnp.where(small >= WIDE * f, e, eastern) if f else e
            western = jnp.where(small >= WIDE * f, w, western) if f else w
        east_out[number] = eastern
        west_out[number] = western
        copies = [up, down]
        for side, (x, source, target) in enumerate(((east, east_out, west_in), (west, west_out, east_in))):
            for y, first, extent, landing in (
                (None, 0, rows, WIDE), (north, rows - WIDE, WIDE, 0), (south, 0, WIDE, WIDE + rows)
            ):
                slot = 6 * number + len(copies) - 2
                copies.append(
                    pltpu.make_async_remote_copy(
                        src_ref=source.at[number, pl.ds(first, extent)],
                        dst_ref=target.at[number, pl.ds(landing, extent)],
                        send_sem=col_send.at[slot], recv_sem=col_recv.at[slot],
                        device_id={"lon": x} if y is None else {"lat": y, "lon": x},
                        device_id_type=MESH,
                    )
                )
                copies[-1].start()
        for copy in copies:
            copy.wait()
        lane = lax.broadcasted_iota(jnp.int32, (high, LANES), 1)
        start = wid - LANES
        own = cols - start
        from_east, from_west = east_in[number], west_in[number]
        for f, fill in enumerate(fills):
            e = pltpu.roll(from_east, (own - WIDE * f) % LANES, 1)
            w = pltpu.roll(from_west, (LANES - WIDE - WIDE * f) % LANES, 1)
            halo = jnp.where(lane < own + WIDE, e, jnp.where(lane >= LANES - WIDE, w, fill))
            if own:
                halo = jnp.where(lane < own, ref[f, :, start:], halo)
            ref[f, :, start:] = halo

    exchange(x_ref, 0, (1.0,) + (0.0,) * 7)

    def below(ref, f, r, extent):
        if r == 0:
            return pltpu.roll(ref[f, :extent, :], 1, 0)
        return pltpu.roll(ref[f, r - TILE : r + extent, :], 1, 0)[TILE:]

    for r in range(0, high, block):
        tall = min(block, high - r)
        here = pl.ds(r, tall)
        d, m, g = x_ref[0, here, :], x_ref[1, here, :], x_ref[2, here, :]
        for side, shifted in enumerate(
            (lambda f, v: pltpu.roll(v, 1, 1), lambda f, v: below(x_ref, f, r, tall))
        ):
            both = d + shifted(0, d)
            wet = m * shifted(1, m)
            st_ref[side, here, :] = wet * (1.0 - (g + shifted(2, g)) / both)
            st_ref[2 + side, here, :] = 0.7 * wet
            st_ref[4 + side, here, :] = 0.3 * both
        st_ref[6, here, :] = m
        st_ref[7, here, :] = m * x_ref[3, here, :]
        st_ref[8, here, :] = m * x_ref[4, here, :]
    gain_ref[0] = x_ref[1, mine, :span]
    for side in range(2):
        g = st_ref[side, mine, :span]
        for _ in range(STEPS.bit_length() - 1):
            g = g * g
        gain_ref[1 + side] = g
    acc_ref[...] = jnp.zeros(acc_ref.shape, jnp.float32)

    def advance(ref, base, offset, extent, first, end, want, t):
        cosine = trig_ref[2 * (k * STEPS + t)]
        sine = trig_ref[2 * (k * STEPS + t) + 1]
        carry = None
        for r in reversed(range(0, extent, block)):
            tall = min(block, extent - r)
            here, there = pl.ds(r, tall), pl.ds(offset + r, tall)
            a = ref[base, here, :]
            p = st_ref[0, there, :] * ref[base + 1, here, :] - st_ref[2, there, :] * (
                a - pltpu.roll(a, 1, 1)
            )
            q = st_ref[1, there, :] * ref[base + 2, here, :] - st_ref[3, there, :] * (
                a - below(ref, base, r, tall)
            )
            u = st_ref[4, there, :] * p
            v = st_ref[5, there, :] * q
            if carry is None:
                v_north = pltpu.roll(v, tall - 1, 0)
            else:
                v_north = pltpu.roll(
                    jnp.concatenate([v, carry], axis=0), tall + TILE - 1, 0
                )[:tall]
            carry = v[:TILE]
            spread = (pltpu.roll(u, wid - 1, 1) - u) + (v_north - v)
            ref[base, here, :] = st_ref[6, there, :] * (a - spread) + (
                st_ref[7, there, :] * cosine + st_ref[8, there, :] * sine
            )
            ref[base + 1, here, :] = p
            ref[base + 2, here, :] = q
            low, top = max(r, first), min(r + tall, end)
            if want and low < top:
                part = pl.ds(offset + low, top - low)
                p, q = p[low - r : top - r], q[low - r : top - r]
                acc_ref[0, part, :] += cosine * p
                acc_ref[1, part, :] += sine * p
                acc_ref[2, part, :] += cosine * q
                acc_ref[3, part, :] += sine * q

    def sweep(ref, base, want, turn, e_ref):
        def keep(source, start, first, extent):
            for f in range(3):
                end_ref[f, pl.ds(first, extent), :] = source[start + f, pl.ds(WIDE, extent), :span]

            @pl.when(k == n - 1)
            def _():
                for f in range(3):
                    e_ref[f, pl.ds(first, extent), :] = source[start + f, pl.ds(WIDE, extent), :span]

        for f in range(3):
            b_ref[f] = ref[base + f, cut:, :]

        def lower(t, nothing):
            advance(ref, base, 0, cut + 2 * WIDE, WIDE, WIDE + cut, want, t)
            return nothing

        lax.fori_loop(0, STEPS, lower, 0)
        keep(ref, base, 0, cut)

        def upper(i, nothing):
            def one(t, nothing):
                advance(b_ref, 0, cut, high - cut, WIDE, WIDE + rows - cut + TILE, want, t)
                return nothing

            lax.fori_loop(i * (STEPS // EARLY), (i + 1) * (STEPS // EARLY), one, 0)
            return turn(i, nothing)

        lax.fori_loop(0, EARLY, upper, 0)
        keep(b_ref, 0, cut, rows - cut)

    half = n // 2
    place = jnp.where(k < half, k, n - 1 - k)
    inner, outer = jnp.where(k < half, later, sooner), jnp.where(k < half, sooner, later)

    def gather():
        return pltpu.make_async_remote_copy(
            src_ref=term_ref, dst_ref=part_ref, send_sem=t_send.at[0], recv_sem=t_recv.at[0],
            device_id={"tm": inner}, device_id_type=MESH,
        )

    def swap():
        return pltpu.make_async_remote_copy(
            src_ref=term_ref, dst_ref=other_ref, send_sem=t_send.at[1], recv_sem=t_recv.at[1],
            device_id={"tm": inner}, device_id_type=MESH,
        )

    def spread_out():
        return pltpu.make_async_remote_copy(
            src_ref=tot_ref, dst_ref=tot_ref, send_sem=t_send.at[2], recv_sem=t_recv.at[2],
            device_id={"tm": outer}, device_id_type=MESH,
        )

    def inward():
        @pl.when(place > 0)
        def _():
            gather().wait_recv()
            term_ref[...] += part_ref[...]

        @pl.when(place < half - 1)
        def _():
            gather().start()

        @pl.when(place == half - 1)
        def _():
            swap().start()

    def outward():
        @pl.when(place == half - 1)
        def _():
            swap().wait_recv()
            tot_ref[...] = term_ref[...] + other_ref[...]

        @pl.when(place < half - 1)
        def _():
            spread_out().wait_recv()

        @pl.when(place > 0)
        def _():
            spread_out().start()

    def settle():
        @pl.when(place < half - 1)
        def _():
            gather().wait_send()

        @pl.when(place == half - 1)
        def _():
            swap().wait_send()

        @pl.when(place > 0)
        def _():
            spread_out().wait_send()

    def relay(number, c_ref, cs_ref, e_ref, want):
        def piece(chunk):
            return pl.ds(pl.multiple_of(chunk * TILE, TILE), TILE)

        def forward(chunk):
            return pltpu.make_async_remote_copy(
                src_ref=cs_ref.at[:, piece(chunk)], dst_ref=c_ref.at[:, piece(chunk)],
                send_sem=c_send.at[number, chunk], recv_sem=c_recv.at[number, chunk],
                device_id={"tm": later}, device_id_type=MESH,
            )

        def back(chunk):
            return pltpu.make_async_remote_copy(
                src_ref=e_ref.at[:, piece(chunk)], dst_ref=e_ref.at[:, piece(chunk)],
                send_sem=e_send.at[number, chunk], recv_sem=e_recv.at[number, chunk],
                device_id={"tm": sooner}, device_id_type=MESH,
            )

        @pl.when(k == 0)
        def _():
            c_ref[...] = jnp.zeros(c_ref.shape, jnp.float32)

        turns = count + SKEW * (n - 1)

        def turn(i, nothing):
            if want:
                pl.when(i == EARLY + 8 * place)(inward)
                pl.when(i == jnp.minimum(EARLY + 8 * (n - 1 - place), turns - 1))(outward)

            ahead = i - SKEW * k

            @pl.when((ahead >= 0) & (ahead < count))
            def _():
                @pl.when(k > 0)
                def _():
                    forward(ahead).wait_recv()

                here = piece(ahead)

                @pl.when(k < n - 1)
                def _():
                    for f in range(3):
                        cs_ref[f, here, :] = end_ref[f, here, :] + gain_ref[f, here, :] * (
                            c_ref[f, here, :] - old_ref[f, here, :]
                        )
                    forward(ahead).start()

            behind = i - SKEW * (n - 1 - k)

            @pl.when((behind >= 0) & (behind < count))
            def _():
                @pl.when(k < n - 1)
                def _():
                    back(behind).wait_recv()

                @pl.when(k > 0)
                def _():
                    back(behind).start()

            return nothing

        def close():
            lax.fori_loop(EARLY, turns, turn, 0)

            for f in range(3):
                power = e_ref[f]
                for j in range(n - 1):
                    power = power * jnp.where(j < k, gain_ref[f], 1.0)
                fresh = c_ref[f] + power
                if want:
                    out_ref[0, f] = fresh[:, :cols]
                else:
                    old_ref[f] = fresh
                    y_ref[f, mine, :span] = fresh

        def sent(chunk, nothing):
            @pl.when(k < n - 1)
            def _():
                forward(chunk).wait_send()

            @pl.when(k > 0)
            def _():
                back(chunk).wait_send()

            return nothing

        return turn, close, lambda: lax.fori_loop(0, count, sent, 0)

    for f in range(3):
        old_ref[f] = x_ref[5 + f, mine, :span]
    turn, close, finish_first = relay(0, c1_ref, cs1_ref, e1_ref, False)
    sweep(x_ref, 5, False, turn, e1_ref)
    close()
    exchange(y_ref, 1, (0.0,) * 3)
    turn, close, finish_second = relay(1, c2_ref, cs2_ref, e2_ref, True)
    sweep(y_ref, 0, True, turn, e2_ref)

    loads[7].wait()
    weight = 0.5 * x_ref[1, mine, :span] / x_ref[0, mine, :span]
    term = jnp.zeros((rows, span), jnp.float32)
    for f in range(4):
        if f < 2:
            v = acc_ref[f, mine, :]
            mid = (v + pltpu.roll(v, wid - 1, 1))[:, :span]
        else:
            v = acc_ref[f, pl.ds(WIDE, rows + TILE), :span]
            mid = (v + pltpu.roll(v, rows + TILE - 1, 0))[:rows]
        flow = flow_ref[f]
        if span > cols:
            flow = jnp.concatenate([flow, jnp.zeros((rows, span - cols), jnp.float32)], axis=1)
        term = term + flow * mid
    term_ref[...] = weight * term

    close()
    grad_ref[...] = tot_ref[:, :cols] * (1.0 / (n * STEPS))
    settle()
    finish_first()
    finish_second()


def shards(
    sizes, depth_class, ocean_mask, depth_levels, drag, tide_force, forward_flow, guess
):
    n = sizes[0]
    rows, cols = ocean_mask.shape
    high = rows + 2 * WIDE
    wid = -(-(cols + 2 * WIDE) // LANES) * LANES
    span = -(-cols // LANES) * LANES
    count = rows // TILE
    assert n % 2 == 0 and count > EARLY and rows % TILE == 0 and rows >= WIDE and wid - LANES <= cols
    counts = np.arange(1, n * STEPS + 1)
    angle = 2.0 * math.pi * counts / (n * STEPS)
    trig = jnp.asarray(np.stack([np.cos(angle), np.sin(angle)], axis=1).reshape(-1), jnp.float32)
    f32 = jnp.float32
    vmem = pl.BlockSpec(memory_space=pltpu.VMEM)
    dma = pltpu.SemaphoreType.DMA
    return pl.pallas_call(
        functools.partial(kernel, sizes),
        out_shape=(
            jax.ShapeDtypeStruct((1, 3, rows, cols), f32),
            jax.ShapeDtypeStruct((rows, cols), f32),
        ),
        in_specs=[pl.BlockSpec(memory_space=pl.ANY)] * 8,
        out_specs=(vmem, vmem),
        scratch_shapes=[
            pltpu.VMEM((rows, cols), jnp.int32),
            pltpu.VMEM((rows, cols), jnp.int32),
            pltpu.SMEM(depth_levels.shape, f32),
            pltpu.VMEM((rows, cols), f32),
            pltpu.VMEM(tide_force.shape, f32),
            pltpu.VMEM(forward_flow.shape, f32),
            pltpu.VMEM(guess.shape, f32),
            pltpu.SMEM(trig.shape, f32),
            dma((8,)),
            pltpu.VMEM((8, high, wid), f32),
            pltpu.VMEM((3, high, wid), f32),
            pltpu.VMEM((3, high - EARLY * TILE, wid), f32),
            pltpu.VMEM((3, rows, span), f32),
            pltpu.VMEM((9, high, wid), f32),
            pltpu.VMEM((4, high, wid), f32),
            pltpu.VMEM((3, rows, span), f32),
            pltpu.VMEM((3, rows, span), f32),
            pltpu.VMEM((rows, span), f32),
            pltpu.VMEM((2, rows, LANES), f32),
            pltpu.VMEM((2, rows, LANES), f32),
            pltpu.VMEM((2, high, LANES), f32),
            pltpu.VMEM((2, high, LANES), f32),
            pltpu.VMEM((3, rows, span), f32),
            pltpu.VMEM((3, rows, span), f32),
            pltpu.VMEM((3, rows, span), f32),
            pltpu.VMEM((3, rows, span), f32),
            pltpu.VMEM((3, rows, span), f32),
            pltpu.VMEM((3, rows, span), f32),
            pltpu.VMEM((rows, span), f32),
            pltpu.VMEM((rows, span), f32),
            pltpu.VMEM((rows, span), f32),
            dma((4,)), dma((4,)), dma((12,)), dma((12,)),
            dma((2, count)), dma((2, count)), dma((2, count)), dma((2, count)),
            dma((3,)), dma((3,)),
        ],
        compiler_params=pltpu.CompilerParams(
            collective_id=0, has_side_effects=True, vmem_limit_bytes=56 * 1024 * 1024
        ),
        name="parareal",
    )(depth_class, ocean_mask, depth_levels, drag, tide_force, forward_flow, guess, trig)


def solution(mesh):
    sizes = tuple(mesh.shape[axis] for axis in ("tm", "lat", "lon"))
    return jax.shard_map(
        functools.partial(shards, sizes),
        mesh=mesh,
        in_specs=(
            P("lat", "lon"),
            P("lat", "lon"),
            P(),
            P("lat", "lon"),
            P(None, "lat", "lon"),
            P(None, "lat", "lon"),
            P("tm", None, "lat", "lon"),
        ),
        out_specs=(P("tm", None, "lat", "lon"), P("lat", "lon")),
        check_vma=False,
    )
```

```python
import functools
import math

import jax
import jax.numpy as jnp
import numpy as np
from jax import lax
from jax.experimental import pallas as pl
from jax.experimental.pallas import tpu as pltpu
from jax.sharding import PartitionSpec as P

STEPS = 16
SWEEPS = 2
DCLASS = 32
WIDE = STEPS
LANES = 128
TILE = 8
EARLY = 8
SKEW = 5

MESH = pl.DeviceIdType.MESH


def kernel(
    sizes, cls_hbm, ocean_hbm, lev_hbm, drag_hbm, force_hbm, flow_hbm, guess_hbm, trig_hbm,
    out_ref, grad_ref,
    cls_ref, ocean_ref, lev_ref, drag_ref, force_ref, flow_ref, guess_ref, trig_ref, load_sem,
    x_ref, y_ref, b_ref, end_ref, st_ref, acc_ref, gain_ref, old_ref, term_ref, east_out, west_out, east_in, west_in,
    c1_ref, cs1_ref, e1_ref, c2_ref, cs2_ref, e2_ref, part_ref, other_ref, tot_ref,
    row_send, row_recv, col_send, col_recv,
    c_send, c_recv, e_send, e_recv, t_send, t_recv,
):
    n, n_lat, n_lon = sizes
    rows, cols = ocean_ref.shape
    high, wid = x_ref.shape[1], x_ref.shape[2]
    span = c1_ref.shape[2]
    block = 2 * TILE
    cut = EARLY * TILE
    mid = cut + 2 * WIDE
    count = rows // TILE
    k, lat, lon = lax.axis_index("tm"), lax.axis_index("lat"), lax.axis_index("lon")
    north, south = lax.rem(lat + 1, n_lat), lax.rem(lat + n_lat - 1, n_lat)
    east, west = lax.rem(lon + 1, n_lon), lax.rem(lon + n_lon - 1, n_lon)
    later, sooner = lax.rem(k + 1, n), lax.rem(k + n - 1, n)

    loads = [
        pltpu.make_async_copy(source, target, load_sem.at[i])
        for i, (source, target) in enumerate((
            (lev_hbm, lev_ref), (cls_hbm, cls_ref), (ocean_hbm, ocean_ref), (drag_hbm, drag_ref),
            (force_hbm, force_ref), (guess_hbm, guess_ref), (trig_hbm, trig_ref), (flow_hbm, flow_ref),
        ))
    ]
    for load in loads:
        load.start()
    barrier = pltpu.get_barrier_semaphore()
    for axis, spot in (
        ("lat", north), ("lat", south), ("lon", east), ("lon", west), ("tm", later), ("tm", sooner)
    ):
        pl.semaphore_signal(barrier, inc=1, device_id={axis: spot}, device_id_type=MESH)
    for y in (north, south):
        for x in (east, west):
            pl.semaphore_signal(barrier, inc=1, device_id={"lat": y, "lon": x}, device_id_type=MESH)

    mine = pl.ds(WIDE, rows)
    loads[0].wait()
    loads[1].wait()
    classes = cls_ref[...]
    depth = jnp.zeros((rows, cols), jnp.float32)
    for c in range(DCLASS):
        depth = jnp.where(classes == c, lev_ref[c], depth)
    x_ref[0, mine, :cols] = depth
    for load in loads[2:7]:
        load.wait()
    line = lat * rows + lax.broadcasted_iota(jnp.int32, (rows, cols), 0)
    polar = (line == 0) | (line == n_lat * rows - 1)
    x_ref[1, mine, :cols] = jnp.where(polar, 0, ocean_ref[...]).astype(jnp.float32)
    x_ref[2, mine, :cols] = drag_ref[...]
    for f in range(2):
        x_ref[3 + f, mine, :cols] = force_ref[f]
    for f in range(3):
        x_ref[5 + f, mine, :cols] = guess_ref[0, f]
        old_ref[f] = x_ref[5 + f, mine, :span]
    pl.semaphore_wait(barrier, 10)

    def exchange(ref, number, fills, moves):
        fields = len(fills)
        low, tops = [], []
        for source, start, skip, landing, extent in moves:
            for copies, y, first, last in (
                (low, north, rows - WIDE, 0), (tops, south, 0, WIDE + rows)
            ):
                slot = 4 * number + len(low) + len(tops)
                copies.append(
                    pltpu.make_async_remote_copy(
                        src_ref=source.at[pl.ds(start, extent), pl.ds(skip + first, WIDE), pl.ds(0, span)],
                        dst_ref=ref.at[pl.ds(landing, extent), pl.ds(last, WIDE), pl.ds(0, span)],
                        send_sem=row_send.at[slot], recv_sem=row_recv.at[slot],
                        device_id={"lat": y}, device_id_type=MESH,
                    )
                )
        for copy in low:
            copy.start()
        small = lax.broadcasted_iota(jnp.int32, (rows, LANES), 1)
        last = (cols - WIDE) // LANES * LANES
        inset = cols - WIDE - last
        eastern = western = None
        for f in range(fields):
            e = pltpu.roll(ref[f, mine, last : last + LANES], (WIDE * f - inset) % LANES, 1)
            w = ref[f, mine, :LANES]
            w = pltpu.roll(w, WIDE * f, 1) if f else w
            eastern = jnp.where(small >= WIDE * f, e, eastern) if f else e
            western = jnp.where(small >= WIDE * f, w, western) if f else w
        east_out[number] = eastern
        west_out[number] = western
        slot = 8 * number
        for x, source, target in ((east, east_out, west_in), (west, west_out, east_in)):
            for copies, y, first, extent, landing in (
                (low, None, 0, mid - WIDE, WIDE), (low, north, rows - WIDE, WIDE, 0),
                (tops, None, mid - WIDE, rows + WIDE - mid, mid), (tops, south, 0, WIDE, WIDE + rows),
            ):
                copies.append(
                    pltpu.make_async_remote_copy(
                        src_ref=source.at[number, pl.ds(first, extent)],
                        dst_ref=target.at[number, pl.ds(landing, extent)],
                        send_sem=col_send.at[slot], recv_sem=col_recv.at[slot],
                        device_id={"lon": x} if y is None else {"lat": y, "lon": x},
                        device_id_type=MESH,
                    )
                )
                slot += 1
        for copy in low[len(moves):] + tops:
            copy.start()

        def settle(copies, first, extent):
            for copy in copies:
                copy.wait()
            lane = lax.broadcasted_iota(jnp.int32, (extent, LANES), 1)
            start = wid - LANES
            own = cols - start
            here = pl.ds(first, extent)
            from_east, from_west = east_in[number, here], west_in[number, here]
            for f, fill in enumerate(fills):
                e = pltpu.roll(from_east, (own - WIDE * f) % LANES, 1)
                w = pltpu.roll(from_west, (LANES - WIDE - WIDE * f) % LANES, 1)
                halo = jnp.where(lane < own + WIDE, e, jnp.where(lane >= LANES - WIDE, w, fill))
                if own:
                    halo = jnp.where(lane < own, ref[f, here, start:], halo)
                ref[f, here, start:] = halo

        settle(low, 0, mid)
        return lambda: settle(tops, mid, high - mid)

    rest = exchange(
        x_ref, 0, (1.0,) + (0.0,) * 7, ((x_ref, 0, WIDE, 0, 5), (old_ref, 0, 0, 5, 3))
    )

    def below(ref, f, r, extent):
        if r == 0:
            return pltpu.roll(ref[f, :extent, :], 1, 0)
        return pltpu.roll(ref[f, r - TILE : r + extent, :], 1, 0)[TILE:]

    def faces(first, last):
        for r in range(first, last, block):
            tall = min(block, last - r)
            here = pl.ds(r, tall)
            d, m, g = x_ref[0, here, :], x_ref[1, here, :], x_ref[2, here, :]
            for side, shifted in enumerate(
                (lambda f, v: pltpu.roll(v, 1, 1), lambda f, v: below(x_ref, f, r, tall))
            ):
                both = d + shifted(0, d)
                wet = m * shifted(1, m)
                st_ref[side, here, :] = wet * (1.0 - (g + shifted(2, g)) / both)
                st_ref[2 + side, here, :] = 0.7 * wet
                st_ref[4 + side, here, :] = 0.3 * both
            st_ref[6, here, :] = m
            st_ref[7, here, :] = m * x_ref[3, here, :]
            st_ref[8, here, :] = m * x_ref[4, here, :]

    def complete():
        rest()
        faces(mid, high)
        gain_ref[0] = x_ref[1, mine, :span]
        for side in range(2):
            g = st_ref[side, mine, :span]
            for _ in range(STEPS.bit_length() - 1):
                g = g * g
            gain_ref[1 + side] = g

    faces(0, mid)
    acc_ref[...] = jnp.zeros(acc_ref.shape, jnp.float32)

    def advance(ref, base, offset, start, stop, first, end, want, t):
        cosine = trig_ref[2 * (k * STEPS + t)]
        sine = trig_ref[2 * (k * STEPS + t) + 1]
        carry = None
        for r in reversed(range(start, stop, block)):
            tall = min(block, stop - r)
            here, there = pl.ds(r, tall), pl.ds(offset + r, tall)
            a = ref[base, here, :]
            p = st_ref[0, there, :] * ref[base + 1, here, :] - st_ref[2, there, :] * (
                a - pltpu.roll(a, 1, 1)
            )
            q = st_ref[1, there, :] * ref[base + 2, here, :] - st_ref[3, there, :] * (
                a - below(ref, base, r, tall)
            )
            u = st_ref[4, there, :] * p
            v = st_ref[5, there, :] * q
            if carry is None:
                v_north = pltpu.roll(v, tall - 1, 0)
            else:
                v_north = pltpu.roll(
                    jnp.concatenate([v, carry], axis=0), tall + TILE - 1, 0
                )[:tall]
            carry = v[:TILE]
            spread = (pltpu.roll(u, wid - 1, 1) - u) + (v_north - v)
            ref[base, here, :] = st_ref[6, there, :] * (a - spread) + (
                st_ref[7, there, :] * cosine + st_ref[8, there, :] * sine
            )
            ref[base + 1, here, :] = p
            ref[base + 2, here, :] = q
            low, top = max(r, first), min(r + tall, end)
            if want and low < top:
                part = pl.ds(offset + low, top - low)
                p, q = p[low - r : top - r], q[low - r : top - r]
                acc_ref[0, part, :] += cosine * p
                acc_ref[1, part, :] += sine * p
                acc_ref[2, part, :] += cosine * q
                acc_ref[3, part, :] += sine * q

    def sweep(ref, base, want, turn, e_ref, between):
        def keep(source, start, first, extent):
            for f in range(3):
                end_ref[f, pl.ds(first, extent), :] = source[start + f, pl.ds(WIDE, extent), :span]

            @pl.when(k == n - 1)
            def _():
                for f in range(3):
                    e_ref[f, pl.ds(first, extent), :] = source[start + f, pl.ds(WIDE, extent), :span]

        for f in range(3):
            b_ref[f, : mid - cut] = ref[base + f, cut:mid, :]

        for trim in (0, TILE):
            def lower(t, nothing):
                advance(ref, base, 0, trim, mid - trim, WIDE, WIDE + cut, want, t)
                return nothing

            begin = STEPS // 2 if trim else 0
            lax.fori_loop(begin, begin + STEPS // 2, lower, 0)
        keep(ref, base, 0, cut)
        between()
        for f in range(3):
            b_ref[f, mid - cut :] = ref[base + f, mid:, :]

        for trim in (0, TILE):
            def upper(i, nothing):
                def one(t, nothing):
                    advance(
                        b_ref, 0, cut, trim, high - cut - trim, WIDE, WIDE + rows - cut + TILE, want, t
                    )
                    return nothing

                lax.fori_loop(i * (STEPS // EARLY), (i + 1) * (STEPS // EARLY), one, 0)
                return turn(i, nothing)

            begin = EARLY // 2 if trim else 0
            lax.fori_loop(begin, begin + EARLY // 2, upper, 0)
        keep(b_ref, 0, cut, rows - cut)

    half = n // 2
    place = jnp.where(k < half, k, n - 1 - k)
    inner, outer = jnp.where(k < half, later, sooner), jnp.where(k < half, sooner, later)

    def gather():
        return pltpu.make_async_remote_copy(
            src_ref=term_ref, dst_ref=part_ref, send_sem=t_send.at[0], recv_sem=t_recv.at[0],
            device_id={"tm": inner}, device_id_type=MESH,
        )

    def swap():
        return pltpu.make_async_remote_copy(
            src_ref=term_ref, dst_ref=other_ref, send_sem=t_send.at[1], recv_sem=t_recv.at[1],
            device_id={"tm": inner}, device_id_type=MESH,
        )

    def spread_out():
        return pltpu.make_async_remote_copy(
            src_ref=tot_ref, dst_ref=tot_ref, send_sem=t_send.at[2], recv_sem=t_recv.at[2],
            device_id={"tm": outer}, device_id_type=MESH,
        )

    def inward():
        @pl.when(place > 0)
        def _():
            gather().wait_recv()
            term_ref[...] += part_ref[...]

        @pl.when(place < half - 1)
        def _():
            gather().start()

        @pl.when(place == half - 1)
        def _():
            swap().start()

    def outward():
        @pl.when(place == half - 1)
        def _():
            swap().wait_recv()
            tot_ref[...] = term_ref[...] + other_ref[...]

        @pl.when(place < half - 1)
        def _():
            spread_out().wait_recv()

        @pl.when(place > 0)
        def _():
            spread_out().start()

    def settle():
        @pl.when(place < half - 1)
        def _():
            gather().wait_send()

        @pl.when(place == half - 1)
        def _():
            swap().wait_send()

        @pl.when(place > 0)
        def _():
            spread_out().wait_send()

    def relay(number, c_ref, cs_ref, e_ref, want):
        def piece(chunk):
            return pl.ds(pl.multiple_of(chunk * TILE, TILE), TILE)

        def forward(chunk):
            return pltpu.make_async_remote_copy(
                src_ref=cs_ref.at[:, piece(chunk)], dst_ref=c_ref.at[:, piece(chunk)],
                send_sem=c_send.at[number, chunk], recv_sem=c_recv.at[number, chunk],
                device_id={"tm": later}, device_id_type=MESH,
            )

        def back(chunk):
            return pltpu.make_async_remote_copy(
                src_ref=e_ref.at[:, piece(chunk)], dst_ref=e_ref.at[:, piece(chunk)],
                send_sem=e_send.at[number, chunk], recv_sem=e_recv.at[number, chunk],
                device_id={"tm": sooner}, device_id_type=MESH,
            )

        @pl.when(k == 0)
        def _():
            c_ref[...] = jnp.zeros(c_ref.shape, jnp.float32)

        turns = count + SKEW * (n - 1)

        def turn(i, nothing):
            if want:
                pl.when(i == EARLY + 8 * place)(inward)
                pl.when(i == jnp.minimum(EARLY + 8 * (n - 1 - place), turns - 1))(outward)

            ahead = i - SKEW * k

            @pl.when((ahead >= 0) & (ahead < count))
            def _():
                @pl.when(k > 0)
                def _():
                    forward(ahead).wait_recv()

                here = piece(ahead)

                @pl.when(k < n - 1)
                def _():
                    for f in range(3):
                        cs_ref[f, here, :] = end_ref[f, here, :] + gain_ref[f, here, :] * (
                            c_ref[f, here, :] - old_ref[f, here, :]
                        )
                    forward(ahead).start()

            behind = i - SKEW * (n - 1 - k)

            @pl.when((behind >= 0) & (behind < count))
            def _():
                @pl.when(k < n - 1)
                def _():
                    back(behind).wait_recv()

                @pl.when(k > 0)
                def _():
                    back(behind).start()

            return nothing

        def close():
            lax.fori_loop(EARLY, turns, turn, 0)

            for f in range(3):
                power = e_ref[f]
                for j in range(n - 1):
                    power = power * jnp.where(j < k, gain_ref[f], 1.0)
                fresh = c_ref[f] + power
                if want:
                    out_ref[0, f] = fresh[:, :cols]
                else:
                    old_ref[f] = fresh
                    y_ref[f, mine, :span] = fresh

        def sent(chunk, nothing):
            @pl.when(k < n - 1)
            def _():
                forward(chunk).wait_send()

            @pl.when(k > 0)
            def _():
                back(chunk).wait_send()

            return nothing

        return turn, close, lambda: lax.fori_loop(0, count, sent, 0)

    turn, close, finish_first = relay(0, c1_ref, cs1_ref, e1_ref, False)
    sweep(x_ref, 5, False, turn, e1_ref, complete)
    close()
    rest_second = exchange(y_ref, 1, (0.0,) * 3, ((old_ref, 0, 0, 0, 3),))
    turn, close, finish_second = relay(1, c2_ref, cs2_ref, e2_ref, True)
    sweep(y_ref, 0, True, turn, e2_ref, rest_second)

    loads[7].wait()
    weight = 0.5 * x_ref[1, mine, :span] / x_ref[0, mine, :span]
    term = jnp.zeros((rows, span), jnp.float32)
    for f in range(4):
        if f < 2:
            v = acc_ref[f, mine, :]
            mid = (v + pltpu.roll(v, wid - 1, 1))[:, :span]
        else:
            v = acc_ref[f, pl.ds(WIDE, rows + TILE), :span]
            mid = (v + pltpu.roll(v, rows + TILE - 1, 0))[:rows]
        flow = flow_ref[f]
        if span > cols:
            flow = jnp.concatenate([flow, jnp.zeros((rows, span - cols), jnp.float32)], axis=1)
        term = term + flow * mid
    term_ref[...] = weight * term

    close()
    grad_ref[...] = tot_ref[:, :cols] * (1.0 / (n * STEPS))
    settle()
    finish_first()
    finish_second()


def shards(
    sizes, depth_class, ocean_mask, depth_levels, drag, tide_force, forward_flow, guess
):
    n = sizes[0]
    rows, cols = ocean_mask.shape
    high = rows + 2 * WIDE
    wid = -(-(cols + 2 * WIDE) // LANES) * LANES
    span = -(-cols // LANES) * LANES
    count = rows // TILE
    assert n % 2 == 0 and count > EARLY and rows % TILE == 0 and rows >= WIDE and wid - LANES <= cols
    counts = np.arange(1, n * STEPS + 1)
    angle = 2.0 * math.pi * counts / (n * STEPS)
    trig = jnp.asarray(np.stack([np.cos(angle), np.sin(angle)], axis=1).reshape(-1), jnp.float32)
    f32 = jnp.float32
    vmem = pl.BlockSpec(memory_space=pltpu.VMEM)
    dma = pltpu.SemaphoreType.DMA
    return pl.pallas_call(
        functools.partial(kernel, sizes),
        out_shape=(
            jax.ShapeDtypeStruct((1, 3, rows, cols), f32),
            jax.ShapeDtypeStruct((rows, cols), f32),
        ),
        in_specs=[pl.BlockSpec(memory_space=pl.ANY)] * 8,
        out_specs=(vmem, vmem),
        scratch_shapes=[
            pltpu.VMEM((rows, cols), jnp.int32),
            pltpu.VMEM((rows, cols), jnp.int32),
            pltpu.SMEM(depth_levels.shape, f32),
            pltpu.VMEM((rows, cols), f32),
            pltpu.VMEM(tide_force.shape, f32),
            pltpu.VMEM(forward_flow.shape, f32),
            pltpu.VMEM(guess.shape, f32),
            pltpu.SMEM(trig.shape, f32),
            dma((8,)),
            pltpu.VMEM((8, high, wid), f32),
            pltpu.VMEM((3, high, wid), f32),
            pltpu.VMEM((3, high - EARLY * TILE, wid), f32),
            pltpu.VMEM((3, rows, span), f32),
            pltpu.VMEM((9, high, wid), f32),
            pltpu.VMEM((4, high, wid), f32),
            pltpu.VMEM((3, rows, span), f32),
            pltpu.VMEM((3, rows, span), f32),
            pltpu.VMEM((rows, span), f32),
            pltpu.VMEM((2, rows, LANES), f32),
            pltpu.VMEM((2, rows, LANES), f32),
            pltpu.VMEM((2, high, LANES), f32),
            pltpu.VMEM((2, high, LANES), f32),
            pltpu.VMEM((3, rows, span), f32),
            pltpu.VMEM((3, rows, span), f32),
            pltpu.VMEM((3, rows, span), f32),
            pltpu.VMEM((3, rows, span), f32),
            pltpu.VMEM((3, rows, span), f32),
            pltpu.VMEM((3, rows, span), f32),
            pltpu.VMEM((rows, span), f32),
            pltpu.VMEM((rows, span), f32),
            pltpu.VMEM((rows, span), f32),
            dma((8,)), dma((8,)), dma((16,)), dma((16,)),
            dma((2, count)), dma((2, count)), dma((2, count)), dma((2, count)),
            dma((3,)), dma((3,)),
        ],
        compiler_params=pltpu.CompilerParams(
            collective_id=0, has_side_effects=True, vmem_limit_bytes=56 * 1024 * 1024
        ),
        name="parareal",
    )(depth_class, ocean_mask, depth_levels, drag, tide_force, forward_flow, guess, trig)


def solution(mesh):
    sizes = tuple(mesh.shape[axis] for axis in ("tm", "lat", "lon"))
    return jax.shard_map(
        functools.partial(shards, sizes),
        mesh=mesh,
        in_specs=(
            P("lat", "lon"),
            P("lat", "lon"),
            P(),
            P("lat", "lon"),
            P(None, "lat", "lon"),
            P(None, "lat", "lon"),
            P("tm", None, "lat", "lon"),
        ),
        out_specs=(P("tm", None, "lat", "lon"), P("lat", "lon")),
        check_vma=False,
    )
```

```python
import functools
import math

import jax
import jax.numpy as jnp
import numpy as np
from jax import lax
from jax.experimental import pallas as pl
from jax.experimental.pallas import tpu as pltpu
from jax.sharding import PartitionSpec as P

STEPS = 16
SWEEPS = 2
DCLASS = 32
WIDE = STEPS
LANES = 128
TILE = 8
EARLY = 8
SKEW = 5

MESH = pl.DeviceIdType.MESH


def kernel(
    sizes, cls_hbm, ocean_hbm, lev_hbm, drag_hbm, force_hbm, flow_hbm, guess_hbm, trig_hbm,
    out_ref, grad_ref,
    cls_ref, ocean_ref, lev_ref, drag_ref, force_ref, flow_ref, guess_ref, trig_ref, load_sem,
    x_ref, y_ref, b_ref, end_ref, st_ref, acc_ref, gain_ref, old_ref, term_ref, east_out, west_out, east_in, west_in,
    c1_ref, cs1_ref, e1_ref, c2_ref, cs2_ref, e2_ref, part_ref, other_ref, tot_ref,
    row_send, row_recv, col_send, col_recv,
    c_send, c_recv, e_send, e_recv, t_send, t_recv,
):
    n, n_lat, n_lon = sizes
    rows, cols = ocean_ref.shape
    high, wid = x_ref.shape[1], x_ref.shape[2]
    span = c1_ref.shape[2]
    block = 2 * TILE
    cut = EARLY * TILE
    mid = cut + 2 * WIDE
    count = rows // TILE
    k, lat, lon = lax.axis_index("tm"), lax.axis_index("lat"), lax.axis_index("lon")
    north, south = lax.rem(lat + 1, n_lat), lax.rem(lat + n_lat - 1, n_lat)
    east, west = lax.rem(lon + 1, n_lon), lax.rem(lon + n_lon - 1, n_lon)
    later, sooner = lax.rem(k + 1, n), lax.rem(k + n - 1, n)

    loads = [
        pltpu.make_async_copy(source, target, load_sem.at[i])
        for i, (source, target) in enumerate((
            (lev_hbm, lev_ref), (cls_hbm, cls_ref), (ocean_hbm, ocean_ref), (drag_hbm, drag_ref),
            (force_hbm, force_ref), (guess_hbm, guess_ref), (trig_hbm, trig_ref), (flow_hbm, flow_ref),
        ))
    ]
    for load in loads:
        load.start()
    barrier = pltpu.get_barrier_semaphore()
    for axis, spot in (
        ("lat", north), ("lat", south), ("lon", east), ("lon", west), ("tm", later), ("tm", sooner)
    ):
        pl.semaphore_signal(barrier, inc=1, device_id={axis: spot}, device_id_type=MESH)
    for y in (north, south):
        for x in (east, west):
            pl.semaphore_signal(barrier, inc=1, device_id={"lat": y, "lon": x}, device_id_type=MESH)

    mine = pl.ds(WIDE, rows)
    loads[0].wait()
    loads[1].wait()
    classes = cls_ref[...]
    depth = jnp.zeros((rows, cols), jnp.float32)
    for c in range(DCLASS):
        depth = jnp.where(classes == c, lev_ref[c], depth)
    x_ref[0, mine, :cols] = depth
    for load in loads[2:7]:
        load.wait()
    line = lat * rows + lax.broadcasted_iota(jnp.int32, (rows, cols), 0)
    polar = (line == 0) | (line == n_lat * rows - 1)
    x_ref[1, mine, :cols] = jnp.where(polar, 0, ocean_ref[...]).astype(jnp.float32)
    x_ref[2, mine, :cols] = drag_ref[...]
    for f in range(2):
        x_ref[3 + f, mine, :cols] = force_ref[f]
    for f in range(3):
        x_ref[5 + f, mine, :cols] = guess_ref[0, f]
        old_ref[f] = x_ref[5 + f, mine, :span]
    pl.semaphore_wait(barrier, 10)

    def exchange(ref, number, fills, moves):
        fields = len(fills)
        low, tops = [], []
        for source, start, skip, landing, extent in moves:
            for copies, y, first, last in (
                (low, north, rows - WIDE, 0), (tops, south, 0, WIDE + rows)
            ):
                slot = 4 * number + len(low) + len(tops)
                copies.append(
                    pltpu.make_async_remote_copy(
                        src_ref=source.at[pl.ds(start, extent), pl.ds(skip + first, WIDE), pl.ds(0, span)],
                        dst_ref=ref.at[pl.ds(landing, extent), pl.ds(last, WIDE), pl.ds(0, span)],
                        send_sem=row_send.at[slot], recv_sem=row_recv.at[slot],
                        device_id={"lat": y}, device_id_type=MESH,
                    )
                )
        for copy in low:
            copy.start()
        small = lax.broadcasted_iota(jnp.int32, (rows, LANES), 1)
        last = (cols - WIDE) // LANES * LANES
        inset = cols - WIDE - last
        eastern = western = None
        for f in range(fields):
            e = pltpu.roll(ref[f, mine, last : last + LANES], (WIDE * f - inset) % LANES, 1)
            w = ref[f, mine, :LANES]
            w = pltpu.roll(w, WIDE * f, 1) if f else w
            eastern = jnp.where(small >= WIDE * f, e, eastern) if f else e
            western = jnp.where(small >= WIDE * f, w, western) if f else w
        east_out[number] = eastern
        west_out[number] = western
        slot = 8 * number
        for x, source, target in ((east, east_out, west_in), (west, west_out, east_in)):
            for copies, y, first, extent, landing in (
                (low, None, 0, mid - WIDE, WIDE), (low, north, rows - WIDE, WIDE, 0),
                (tops, None, mid - WIDE, rows + WIDE - mid, mid), (tops, south, 0, WIDE, WIDE + rows),
            ):
                copies.append(
                    pltpu.make_async_remote_copy(
                        src_ref=source.at[number, pl.ds(first, extent)],
                        dst_ref=target.at[number, pl.ds(landing, extent)],
                        send_sem=col_send.at[slot], recv_sem=col_recv.at[slot],
                        device_id={"lon": x} if y is None else {"lat": y, "lon": x},
                        device_id_type=MESH,
                    )
                )
                slot += 1
        for copy in low[len(moves):] + tops:
            copy.start()

        def settle(copies, first, extent):
            for copy in copies:
                copy.wait()
            lane = lax.broadcasted_iota(jnp.int32, (extent, LANES), 1)
            start = wid - LANES
            own = cols - start
            here = pl.ds(first, extent)
            from_east, from_west = east_in[number, here], west_in[number, here]
            for f, fill in enumerate(fills):
                e = pltpu.roll(from_east, (own - WIDE * f) % LANES, 1)
                w = pltpu.roll(from_west, (LANES - WIDE - WIDE * f) % LANES, 1)
                halo = jnp.where(lane < own + WIDE, e, jnp.where(lane >= LANES - WIDE, w, fill))
                if own:
                    halo = jnp.where(lane < own, ref[f, here, start:], halo)
                ref[f, here, start:] = halo

        settle(low, 0, mid)
        return lambda: settle(tops, mid, high - mid)

    rest = exchange(
        x_ref, 0, (1.0,) + (0.0,) * 7, ((x_ref, 0, WIDE, 0, 5), (old_ref, 0, 0, 5, 3))
    )

    def below(ref, f, r, extent):
        if r == 0:
            return pltpu.roll(ref[f, :extent, :], 1, 0)
        return pltpu.roll(ref[f, r - TILE : r + extent, :], 1, 0)[TILE:]

    def faces(first, last):
        for r in range(first, last, block):
            tall = min(block, last - r)
            here = pl.ds(r, tall)
            d, m, g = x_ref[0, here, :], x_ref[1, here, :], x_ref[2, here, :]
            for side, shifted in enumerate(
                (lambda f, v: pltpu.roll(v, 1, 1), lambda f, v: below(x_ref, f, r, tall))
            ):
                both = d + shifted(0, d)
                wet = m * shifted(1, m)
                st_ref[side, here, :] = wet * (1.0 - (g + shifted(2, g)) / both)
                st_ref[2 + side, here, :] = 0.7 * wet
                st_ref[4 + side, here, :] = 0.3 * both
            st_ref[6, here, :] = m
            st_ref[7, here, :] = m * x_ref[3, here, :]
            st_ref[8, here, :] = m * x_ref[4, here, :]

    def complete():
        rest()
        faces(mid, high)
        gain_ref[0] = x_ref[1, mine, :span]
        for side in range(2):
            g = st_ref[side, mine, :span]
            for _ in range(STEPS.bit_length() - 1):
                g = g * g
            gain_ref[1 + side] = g

    faces(0, mid)
    acc_ref[...] = jnp.zeros(acc_ref.shape, jnp.float32)

    def advance(ref, base, offset, start, stop, first, end, want, t):
        cosine = trig_ref[2 * (k * STEPS + t)]
        sine = trig_ref[2 * (k * STEPS + t) + 1]
        line = lax.broadcasted_iota(jnp.int32, (TILE, wid), 0)
        a = ref[base, stop - TILE : stop, :]
        a_turned = pltpu.roll(a, 1, 0)
        v_above = None
        for r in reversed(range(start, stop, TILE)):
            tall = TILE
            here, there = pl.ds(r, TILE), pl.ds(offset + r, TILE)
            if r >= TILE:
                a_next = ref[base, r - TILE : r, :]
                next_turned = pltpu.roll(a_next, 1, 0)
                a_south = jnp.where(line == 0, next_turned, a_turned)
            else:
                a_next, next_turned, a_south = a, a_turned, a_turned
            p = st_ref[0, there, :] * ref[base + 1, here, :] - st_ref[2, there, :] * (
                a - pltpu.roll(a, 1, 1)
            )
            q = st_ref[1, there, :] * ref[base + 2, here, :] - st_ref[3, there, :] * (a - a_south)
            u = st_ref[4, there, :] * p
            v = st_ref[5, there, :] * q
            v_turned = pltpu.roll(v, TILE - 1, 0)
            v_north = v_turned if v_above is None else jnp.where(line == TILE - 1, v_above, v_turned)
            v_above = v_turned
            spread = (pltpu.roll(u, wid - 1, 1) - u) + (v_north - v)
            ref[base, here, :] = st_ref[6, there, :] * (a - spread) + (
                st_ref[7, there, :] * cosine + st_ref[8, there, :] * sine
            )
            ref[base + 1, here, :] = p
            ref[base + 2, here, :] = q
            a, a_turned = a_next, next_turned
            low, top = max(r, first), min(r + tall, end)
            if want and low < top:
                part = pl.ds(offset + low, top - low)
                p, q = p[low - r : top - r], q[low - r : top - r]
                acc_ref[0, part, :] += cosine * p
                acc_ref[1, part, :] += sine * p
                acc_ref[2, part, :] += cosine * q
                acc_ref[3, part, :] += sine * q

    def sweep(ref, base, want, turn, e_ref, between):
        def keep(source, start, first, extent):
            for f in range(3):
                end_ref[f, pl.ds(first, extent), :] = source[start + f, pl.ds(WIDE, extent), :span]

            @pl.when(k == n - 1)
            def _():
                for f in range(3):
                    e_ref[f, pl.ds(first, extent), :] = source[start + f, pl.ds(WIDE, extent), :span]

        for f in range(3):
            b_ref[f, : mid - cut] = ref[base + f, cut:mid, :]

        for trim in (0, TILE):
            def lower(t, nothing):
                advance(ref, base, 0, trim, mid - trim, WIDE, WIDE + cut, want, t)
                return nothing

            begin = STEPS // 2 if trim else 0
            lax.fori_loop(begin, begin + STEPS // 2, lower, 0)
        keep(ref, base, 0, cut)
        between()
        for f in range(3):
            b_ref[f, mid - cut :] = ref[base + f, mid:, :]

        for trim in (0, TILE):
            def upper(i, nothing):
                def one(t, nothing):
                    advance(
                        b_ref, 0, cut, trim, high - cut - trim, WIDE, WIDE + rows - cut + TILE, want, t
                    )
                    return nothing

                lax.fori_loop(i * (STEPS // EARLY), (i + 1) * (STEPS // EARLY), one, 0)
                return turn(i, nothing)

            begin = EARLY // 2 if trim else 0
            lax.fori_loop(begin, begin + EARLY // 2, upper, 0)
        keep(b_ref, 0, cut, rows - cut)

    half = n // 2
    place = jnp.where(k < half, k, n - 1 - k)
    inner, outer = jnp.where(k < half, later, sooner), jnp.where(k < half, sooner, later)

    def gather():
        return pltpu.make_async_remote_copy(
            src_ref=term_ref, dst_ref=part_ref, send_sem=t_send.at[0], recv_sem=t_recv.at[0],
            device_id={"tm": inner}, device_id_type=MESH,
        )

    def swap():
        return pltpu.make_async_remote_copy(
            src_ref=term_ref, dst_ref=other_ref, send_sem=t_send.at[1], recv_sem=t_recv.at[1],
            device_id={"tm": inner}, device_id_type=MESH,
        )

    def spread_out():
        return pltpu.make_async_remote_copy(
            src_ref=tot_ref, dst_ref=tot_ref, send_sem=t_send.at[2], recv_sem=t_recv.at[2],
            device_id={"tm": outer}, device_id_type=MESH,
        )

    def inward():
        @pl.when(place > 0)
        def _():
            gather().wait_recv()
            term_ref[...] += part_ref[...]

        @pl.when(place < half - 1)
        def _():
            gather().start()

        @pl.when(place == half - 1)
        def _():
            swap().start()

    def outward():
        @pl.when(place == half - 1)
        def _():
            swap().wait_recv()
            tot_ref[...] = term_ref[...] + other_ref[...]

        @pl.when(place < half - 1)
        def _():
            spread_out().wait_recv()

        @pl.when(place > 0)
        def _():
            spread_out().start()

    def settle():
        @pl.when(place < half - 1)
        def _():
            gather().wait_send()

        @pl.when(place == half - 1)
        def _():
            swap().wait_send()

        @pl.when(place > 0)
        def _():
            spread_out().wait_send()

    def relay(number, c_ref, cs_ref, e_ref, want):
        def piece(chunk):
            return pl.ds(pl.multiple_of(chunk * TILE, TILE), TILE)

        def forward(chunk):
            return pltpu.make_async_remote_copy(
                src_ref=cs_ref.at[:, piece(chunk)], dst_ref=c_ref.at[:, piece(chunk)],
                send_sem=c_send.at[number, chunk], recv_sem=c_recv.at[number, chunk],
                device_id={"tm": later}, device_id_type=MESH,
            )

        def back(chunk):
            return pltpu.make_async_remote_copy(
                src_ref=e_ref.at[:, piece(chunk)], dst_ref=e_ref.at[:, piece(chunk)],
                send_sem=e_send.at[number, chunk], recv_sem=e_recv.at[number, chunk],
                device_id={"tm": sooner}, device_id_type=MESH,
            )

        @pl.when(k == 0)
        def _():
            c_ref[...] = jnp.zeros(c_ref.shape, jnp.float32)

        turns = count + SKEW * (n - 1)

        def turn(i, nothing):
            if want:
                pl.when(i == EARLY + 8 * place)(inward)
                pl.when(i == jnp.minimum(EARLY + 8 * (n - 1 - place), turns - 1))(outward)

            ahead = i - SKEW * k

            @pl.when((ahead >= 0) & (ahead < count))
            def _():
                @pl.when(k > 0)
                def _():
                    forward(ahead).wait_recv()

                here = piece(ahead)

                @pl.when(k < n - 1)
                def _():
                    for f in range(3):
                        cs_ref[f, here, :] = end_ref[f, here, :] + gain_ref[f, here, :] * (
                            c_ref[f, here, :] - old_ref[f, here, :]
                        )
                    forward(ahead).start()

            behind = i - SKEW * (n - 1 - k)

            @pl.when((behind >= 0) & (behind < count))
            def _():
                @pl.when(k < n - 1)
                def _():
                    back(behind).wait_recv()

                @pl.when(k > 0)
                def _():
                    back(behind).start()

            return nothing

        def close():
            lax.fori_loop(EARLY, turns, turn, 0)

            for f in range(3):
                power = e_ref[f]
                for j in range(n - 1):
                    power = power * jnp.where(j < k, gain_ref[f], 1.0)
                fresh = c_ref[f] + power
                if want:
                    out_ref[0, f] = fresh[:, :cols]
                else:
                    old_ref[f] = fresh
                    y_ref[f, mine, :span] = fresh

        def sent(chunk, nothing):
            @pl.when(k < n - 1)
            def _():
                forward(chunk).wait_send()

            @pl.when(k > 0)
            def _():
                back(chunk).wait_send()

            return nothing

        return turn, close, lambda: lax.fori_loop(0, count, sent, 0)

    turn, close, finish_first = relay(0, c1_ref, cs1_ref, e1_ref, False)
    sweep(x_ref, 5, False, turn, e1_ref, complete)
    close()
    rest_second = exchange(y_ref, 1, (0.0,) * 3, ((old_ref, 0, 0, 0, 3),))
    turn, close, finish_second = relay(1, c2_ref, cs2_ref, e2_ref, True)
    sweep(y_ref, 0, True, turn, e2_ref, rest_second)

    loads[7].wait()
    weight = 0.5 * x_ref[1, mine, :span] / x_ref[0, mine, :span]
    term = jnp.zeros((rows, span), jnp.float32)
    for f in range(4):
        if f < 2:
            v = acc_ref[f, mine, :]
            mid = (v + pltpu.roll(v, wid - 1, 1))[:, :span]
        else:
            v = acc_ref[f, pl.ds(WIDE, rows + TILE), :span]
            mid = (v + pltpu.roll(v, rows + TILE - 1, 0))[:rows]
        flow = flow_ref[f]
        if span > cols:
            flow = jnp.concatenate([flow, jnp.zeros((rows, span - cols), jnp.float32)], axis=1)
        term = term + flow * mid
    term_ref[...] = weight * term

    close()
    grad_ref[...] = tot_ref[:, :cols] * (1.0 / (n * STEPS))
    settle()
    finish_first()
    finish_second()


def shards(
    sizes, depth_class, ocean_mask, depth_levels, drag, tide_force, forward_flow, guess
):
    n = sizes[0]
    rows, cols = ocean_mask.shape
    high = rows + 2 * WIDE
    wid = -(-(cols + 2 * WIDE) // LANES) * LANES
    span = -(-cols // LANES) * LANES
    count = rows // TILE
    assert n % 2 == 0 and count > EARLY and rows % TILE == 0 and rows >= WIDE and wid - LANES <= cols
    counts = np.arange(1, n * STEPS + 1)
    angle = 2.0 * math.pi * counts / (n * STEPS)
    trig = jnp.asarray(np.stack([np.cos(angle), np.sin(angle)], axis=1).reshape(-1), jnp.float32)
    f32 = jnp.float32
    vmem = pl.BlockSpec(memory_space=pltpu.VMEM)
    dma = pltpu.SemaphoreType.DMA
    return pl.pallas_call(
        functools.partial(kernel, sizes),
        out_shape=(
            jax.ShapeDtypeStruct((1, 3, rows, cols), f32),
            jax.ShapeDtypeStruct((rows, cols), f32),
        ),
        in_specs=[pl.BlockSpec(memory_space=pl.ANY)] * 8,
        out_specs=(vmem, vmem),
        scratch_shapes=[
            pltpu.VMEM((rows, cols), jnp.int32),
            pltpu.VMEM((rows, cols), jnp.int32),
            pltpu.SMEM(depth_levels.shape, f32),
            pltpu.VMEM((rows, cols), f32),
            pltpu.VMEM(tide_force.shape, f32),
            pltpu.VMEM(forward_flow.shape, f32),
            pltpu.VMEM(guess.shape, f32),
            pltpu.SMEM(trig.shape, f32),
            dma((8,)),
            pltpu.VMEM((8, high, wid), f32),
            pltpu.VMEM((3, high, wid), f32),
            pltpu.VMEM((3, high - EARLY * TILE, wid), f32),
            pltpu.VMEM((3, rows, span), f32),
            pltpu.VMEM((9, high, wid), f32),
            pltpu.VMEM((4, high, wid), f32),
            pltpu.VMEM((3, rows, span), f32),
            pltpu.VMEM((3, rows, span), f32),
            pltpu.VMEM((rows, span), f32),
            pltpu.VMEM((2, rows, LANES), f32),
            pltpu.VMEM((2, rows, LANES), f32),
            pltpu.VMEM((2, high, LANES), f32),
            pltpu.VMEM((2, high, LANES), f32),
            pltpu.VMEM((3, rows, span), f32),
            pltpu.VMEM((3, rows, span), f32),
            pltpu.VMEM((3, rows, span), f32),
            pltpu.VMEM((3, rows, span), f32),
            pltpu.VMEM((3, rows, span), f32),
            pltpu.VMEM((3, rows, span), f32),
            pltpu.VMEM((rows, span), f32),
            pltpu.VMEM((rows, span), f32),
            pltpu.VMEM((rows, span), f32),
            dma((8,)), dma((8,)), dma((16,)), dma((16,)),
            dma((2, count)), dma((2, count)), dma((2, count)), dma((2, count)),
            dma((3,)), dma((3,)),
        ],
        compiler_params=pltpu.CompilerParams(
            collective_id=0, has_side_effects=True, vmem_limit_bytes=56 * 1024 * 1024
        ),
        name="parareal",
    )(depth_class, ocean_mask, depth_levels, drag, tide_force, forward_flow, guess, trig)


def solution(mesh):
    sizes = tuple(mesh.shape[axis] for axis in ("tm", "lat", "lon"))
    return jax.shard_map(
        functools.partial(shards, sizes),
        mesh=mesh,
        in_specs=(
            P("lat", "lon"),
            P("lat", "lon"),
            P(),
            P("lat", "lon"),
            P(None, "lat", "lon"),
            P(None, "lat", "lon"),
            P("tm", None, "lat", "lon"),
        ),
        out_specs=(P("tm", None, "lat", "lon"), P("lat", "lon")),
        check_vma=False,
    )
```

```python
import functools
import math

import jax
import jax.numpy as jnp
import numpy as np
from jax import lax
from jax.experimental import pallas as pl
from jax.experimental.pallas import tpu as pltpu
from jax.sharding import PartitionSpec as P

STEPS = 16
SWEEPS = 2
DCLASS = 32
WIDE = STEPS
LANES = 128
TILE = 8
EARLY = 8
SKEW = 4

MESH = pl.DeviceIdType.MESH


def kernel(
    sizes, cls_hbm, ocean_hbm, lev_hbm, drag_hbm, force_hbm, flow_hbm, guess_hbm, trig_hbm,
    out_ref, grad_ref,
    cls_ref, ocean_ref, lev_ref, drag_ref, force_ref, flow_ref, guess_ref, trig_ref, load_sem,
    x_ref, y_ref, b_ref, end_ref, st_ref, acc_ref, gain_ref, old_ref, term_ref, east_out, west_out, east_in, west_in,
    c1_ref, cs1_ref, e1_ref, c2_ref, cs2_ref, e2_ref, part_ref, other_ref, tot_ref,
    row_send, row_recv, col_send, col_recv,
    c_send, c_recv, e_send, e_recv, t_send, t_recv,
):
    n, n_lat, n_lon = sizes
    rows, cols = ocean_ref.shape
    high, wid = x_ref.shape[1], x_ref.shape[2]
    span = c1_ref.shape[2]
    block = 2 * TILE
    cut = EARLY * TILE
    mid = cut + 2 * WIDE
    count = rows // TILE
    k, lat, lon = lax.axis_index("tm"), lax.axis_index("lat"), lax.axis_index("lon")
    north, south = lax.rem(lat + 1, n_lat), lax.rem(lat + n_lat - 1, n_lat)
    east, west = lax.rem(lon + 1, n_lon), lax.rem(lon + n_lon - 1, n_lon)
    later, sooner = lax.rem(k + 1, n), lax.rem(k + n - 1, n)

    loads = [
        pltpu.make_async_copy(source, target, load_sem.at[i])
        for i, (source, target) in enumerate((
            (lev_hbm, lev_ref), (cls_hbm, cls_ref), (ocean_hbm, ocean_ref), (drag_hbm, drag_ref),
            (force_hbm, force_ref), (guess_hbm, guess_ref), (trig_hbm, trig_ref), (flow_hbm, flow_ref),
        ))
    ]
    for load in loads:
        load.start()
    barrier = pltpu.get_barrier_semaphore()
    for axis, spot in (
        ("lat", north), ("lat", south), ("lon", east), ("lon", west), ("tm", later), ("tm", sooner)
    ):
        pl.semaphore_signal(barrier, inc=1, device_id={axis: spot}, device_id_type=MESH)
    for y in (north, south):
        for x in (east, west):
            pl.semaphore_signal(barrier, inc=1, device_id={"lat": y, "lon": x}, device_id_type=MESH)

    mine = pl.ds(WIDE, rows)
    loads[0].wait()
    loads[1].wait()
    classes = cls_ref[...]
    depth = jnp.zeros((rows, cols), jnp.float32)
    for c in range(DCLASS):
        depth = jnp.where(classes == c, lev_ref[c], depth)
    x_ref[0, mine, :cols] = depth
    for load in loads[2:7]:
        load.wait()
    line = lat * rows + lax.broadcasted_iota(jnp.int32, (rows, cols), 0)
    polar = (line == 0) | (line == n_lat * rows - 1)
    x_ref[1, mine, :cols] = jnp.where(polar, 0, ocean_ref[...]).astype(jnp.float32)
    x_ref[2, mine, :cols] = drag_ref[...]
    for f in range(2):
        x_ref[3 + f, mine, :cols] = force_ref[f]
    for f in range(3):
        x_ref[5 + f, mine, :cols] = guess_ref[0, f]
        old_ref[f] = x_ref[5 + f, mine, :span]
    pl.semaphore_wait(barrier, 10)

    def exchange(ref, number, fills, moves):
        fields = len(fills)
        low, tops = [], []
        for source, start, skip, landing, extent in moves:
            for copies, y, first, last in (
                (low, north, rows - WIDE, 0), (tops, south, 0, WIDE + rows)
            ):
                slot = 4 * number + len(low) + len(tops)
                copies.append(
                    pltpu.make_async_remote_copy(
                        src_ref=source.at[pl.ds(start, extent), pl.ds(skip + first, WIDE), pl.ds(0, span)],
                        dst_ref=ref.at[pl.ds(landing, extent), pl.ds(last, WIDE), pl.ds(0, span)],
                        send_sem=row_send.at[slot], recv_sem=row_recv.at[slot],
                        device_id={"lat": y}, device_id_type=MESH,
                    )
                )
        for copy in low:
            copy.start()
        small = lax.broadcasted_iota(jnp.int32, (rows, LANES), 1)
        last = (cols - WIDE) // LANES * LANES
        inset = cols - WIDE - last
        eastern = western = None
        for f in range(fields):
            e = pltpu.roll(ref[f, mine, last : last + LANES], (WIDE * f - inset) % LANES, 1)
            w = ref[f, mine, :LANES]
            w = pltpu.roll(w, WIDE * f, 1) if f else w
            eastern = jnp.where(small >= WIDE * f, e, eastern) if f else e
            western = jnp.where(small >= WIDE * f, w, western) if f else w
        east_out[number] = eastern
        west_out[number] = western
        slot = 8 * number
        for x, source, target in ((east, east_out, west_in), (west, west_out, east_in)):
            for copies, y, first, extent, landing in (
                (low, None, 0, mid - WIDE, WIDE), (low, north, rows - WIDE, WIDE, 0),
                (tops, None, mid - WIDE, rows + WIDE - mid, mid), (tops, south, 0, WIDE, WIDE + rows),
            ):
                copies.append(
                    pltpu.make_async_remote_copy(
                        src_ref=source.at[number, pl.ds(first, extent)],
                        dst_ref=target.at[number, pl.ds(landing, extent)],
                        send_sem=col_send.at[slot], recv_sem=col_recv.at[slot],
                        device_id={"lon": x} if y is None else {"lat": y, "lon": x},
                        device_id_type=MESH,
                    )
                )
                slot += 1
        for copy in low[len(moves):] + tops:
            copy.start()

        def settle(copies, first, extent):
            for copy in copies:
                copy.wait()
            lane = lax.broadcasted_iota(jnp.int32, (extent, LANES), 1)
            start = wid - LANES
            own = cols - start
            here = pl.ds(first, extent)
            from_east, from_west = east_in[number, here], west_in[number, here]
            for f, fill in enumerate(fills):
                e = pltpu.roll(from_east, (own - WIDE * f) % LANES, 1)
                w = pltpu.roll(from_west, (LANES - WIDE - WIDE * f) % LANES, 1)
                halo = jnp.where(lane < own + WIDE, e, jnp.where(lane >= LANES - WIDE, w, fill))
                if own:
                    halo = jnp.where(lane < own, ref[f, here, start:], halo)
                ref[f, here, start:] = halo

        settle(low, 0, mid)
        return lambda: settle(tops, mid, high - mid)

    rest = exchange(
        x_ref, 0, (1.0,) + (0.0,) * 7, ((x_ref, 0, WIDE, 0, 5), (old_ref, 0, 0, 5, 3))
    )

    def below(ref, f, r, extent):
        if r == 0:
            return pltpu.roll(ref[f, :extent, :], 1, 0)
        return pltpu.roll(ref[f, r - TILE : r + extent, :], 1, 0)[TILE:]

    def faces(first, last):
        for r in range(first, last, block):
            tall = min(block, last - r)
            here = pl.ds(r, tall)
            d, m, g = x_ref[0, here, :], x_ref[1, here, :], x_ref[2, here, :]
            for side, shifted in enumerate(
                (lambda f, v: pltpu.roll(v, 1, 1), lambda f, v: below(x_ref, f, r, tall))
            ):
                both = d + shifted(0, d)
                wet = m * shifted(1, m)
                st_ref[side, here, :] = wet * (1.0 - (g + shifted(2, g)) / both)
                st_ref[2 + side, here, :] = 0.7 * wet
                st_ref[4 + side, here, :] = 0.3 * both
            st_ref[6, here, :] = m
            st_ref[7, here, :] = m * x_ref[3, here, :]
            st_ref[8, here, :] = m * x_ref[4, here, :]

    def complete():
        rest()
        faces(mid, high)
        gain_ref[0] = x_ref[1, mine, :span]
        for side in range(2):
            g = st_ref[side, mine, :span]
            for _ in range(STEPS.bit_length() - 1):
                g = g * g
            gain_ref[1 + side] = g

    faces(0, mid)
    acc_ref[...] = jnp.zeros(acc_ref.shape, jnp.float32)

    def advance(ref, base, offset, start, stop, first, end, want, t):
        cosine = trig_ref[2 * (k * STEPS + t)]
        sine = trig_ref[2 * (k * STEPS + t) + 1]
        carry = None
        for r in reversed(range(start, stop, block)):
            tall = min(block, stop - r)
            here, there = pl.ds(r, tall), pl.ds(offset + r, tall)
            a = ref[base, here, :]
            p = st_ref[0, there, :] * ref[base + 1, here, :] - st_ref[2, there, :] * (
                a - pltpu.roll(a, 1, 1)
            )
            q = st_ref[1, there, :] * ref[base + 2, here, :] - st_ref[3, there, :] * (
                a - below(ref, base, r, tall)
            )
            u = st_ref[4, there, :] * p
            v = st_ref[5, there, :] * q
            if carry is None:
                v_north = pltpu.roll(v, tall - 1, 0)
            else:
                v_north = pltpu.roll(
                    jnp.concatenate([v, carry], axis=0), tall + TILE - 1, 0
                )[:tall]
            carry = v[:TILE]
            spread = (pltpu.roll(u, wid - 1, 1) - u) + (v_north - v)
            ref[base, here, :] = st_ref[6, there, :] * (a - spread) + (
                st_ref[7, there, :] * cosine + st_ref[8, there, :] * sine
            )
            ref[base + 1, here, :] = p
            ref[base + 2, here, :] = q
            low, top = max(r, first), min(r + tall, end)
            if want and low < top:
                part = pl.ds(offset + low, top - low)
                p, q = p[low - r : top - r], q[low - r : top - r]
                acc_ref[0, part, :] += cosine * p
                acc_ref[1, part, :] += sine * p
                acc_ref[2, part, :] += cosine * q
                acc_ref[3, part, :] += sine * q

    def sweep(ref, base, want, turn, e_ref, between):
        def keep(source, start, first, extent):
            for f in range(3):
                end_ref[f, pl.ds(first, extent), :] = source[start + f, pl.ds(WIDE, extent), :span]

            @pl.when(k == n - 1)
            def _():
                for f in range(3):
                    e_ref[f, pl.ds(first, extent), :] = source[start + f, pl.ds(WIDE, extent), :span]

        for f in range(3):
            b_ref[f, : mid - cut] = ref[base + f, cut:mid, :]

        for trim in (0, TILE):
            def lower(t, nothing):
                advance(ref, base, 0, trim, mid - trim, WIDE, WIDE + cut, want, t)
                return nothing

            begin = STEPS // 2 if trim else 0
            lax.fori_loop(begin, begin + STEPS // 2, lower, 0)
        keep(ref, base, 0, cut)
        between()
        for f in range(3):
            b_ref[f, mid - cut :] = ref[base + f, mid:, :]

        for trim in (0, TILE):
            def upper(i, nothing):
                def one(t, nothing):
                    advance(
                        b_ref, 0, cut, trim, high - cut - trim, WIDE, WIDE + rows - cut + TILE, want, t
                    )
                    return nothing

                lax.fori_loop(i * (STEPS // EARLY), (i + 1) * (STEPS // EARLY), one, 0)
                return turn(i, nothing)

            begin = EARLY // 2 if trim else 0
            lax.fori_loop(begin, begin + EARLY // 2, upper, 0)
        keep(b_ref, 0, cut, rows - cut)

    half = n // 2
    place = jnp.where(k < half, k, n - 1 - k)
    inner, outer = jnp.where(k < half, later, sooner), jnp.where(k < half, sooner, later)

    def gather():
        return pltpu.make_async_remote_copy(
            src_ref=term_ref, dst_ref=part_ref, send_sem=t_send.at[0], recv_sem=t_recv.at[0],
            device_id={"tm": inner}, device_id_type=MESH,
        )

    def swap():
        return pltpu.make_async_remote_copy(
            src_ref=term_ref, dst_ref=other_ref, send_sem=t_send.at[1], recv_sem=t_recv.at[1],
            device_id={"tm": inner}, device_id_type=MESH,
        )

    def spread_out():
        return pltpu.make_async_remote_copy(
            src_ref=tot_ref, dst_ref=tot_ref, send_sem=t_send.at[2], recv_sem=t_recv.at[2],
            device_id={"tm": outer}, device_id_type=MESH,
        )

    def inward():
        @pl.when(place > 0)
        def _():
            gather().wait_recv()
            term_ref[...] += part_ref[...]

        @pl.when(place < half - 1)
        def _():
            gather().start()

        @pl.when(place == half - 1)
        def _():
            swap().start()

    def outward():
        @pl.when(place == half - 1)
        def _():
            swap().wait_recv()
            tot_ref[...] = term_ref[...] + other_ref[...]

        @pl.when(place < half - 1)
        def _():
            spread_out().wait_recv()

        @pl.when(place > 0)
        def _():
            spread_out().start()

    def settle():
        @pl.when(place < half - 1)
        def _():
            gather().wait_send()

        @pl.when(place == half - 1)
        def _():
            swap().wait_send()

        @pl.when(place > 0)
        def _():
            spread_out().wait_send()

    def relay(number, c_ref, cs_ref, e_ref, want):
        def piece(chunk):
            return pl.ds(pl.multiple_of(chunk * TILE, TILE), TILE)

        def forward(chunk):
            return pltpu.make_async_remote_copy(
                src_ref=cs_ref.at[:, piece(chunk)], dst_ref=c_ref.at[:, piece(chunk)],
                send_sem=c_send.at[number, chunk], recv_sem=c_recv.at[number, chunk],
                device_id={"tm": later}, device_id_type=MESH,
            )

        def back(chunk):
            return pltpu.make_async_remote_copy(
                src_ref=e_ref.at[:, piece(chunk)], dst_ref=e_ref.at[:, piece(chunk)],
                send_sem=e_send.at[number, chunk], recv_sem=e_recv.at[number, chunk],
                device_id={"tm": sooner}, device_id_type=MESH,
            )

        @pl.when(k == 0)
        def _():
            c_ref[...] = jnp.zeros(c_ref.shape, jnp.float32)

        turns = count + SKEW * (n - 1)

        def turn(i, nothing):
            if want:
                pl.when(i == EARLY + 8 * place)(inward)
                pl.when(i == jnp.minimum(EARLY + 8 * (n - 1 - place), turns - 1))(outward)

            ahead = i - SKEW * k

            @pl.when((ahead >= 0) & (ahead < count))
            def _():
                @pl.when(k > 0)
                def _():
                    forward(ahead).wait_recv()

                here = piece(ahead)

                @pl.when(k < n - 1)
                def _():
                    for f in range(3):
                        cs_ref[f, here, :] = end_ref[f, here, :] + gain_ref[f, here, :] * (
                            c_ref[f, here, :] - old_ref[f, here, :]
                        )
                    forward(ahead).start()

            behind = i - SKEW * (n - 1 - k)

            @pl.when((behind >= 0) & (behind < count))
            def _():
                @pl.when(k < n - 1)
                def _():
                    back(behind).wait_recv()

                @pl.when(k > 0)
                def _():
                    back(behind).start()

            return nothing

        def close():
            lax.fori_loop(EARLY, turns, turn, 0)

            for f in range(3):
                power = e_ref[f]
                for j in range(n - 1):
                    power = power * jnp.where(j < k, gain_ref[f], 1.0)
                fresh = c_ref[f] + power
                if want:
                    out_ref[0, f] = fresh[:, :cols]
                else:
                    old_ref[f] = fresh
                    y_ref[f, mine, :span] = fresh

        def sent(chunk, nothing):
            @pl.when(k < n - 1)
            def _():
                forward(chunk).wait_send()

            @pl.when(k > 0)
            def _():
                back(chunk).wait_send()

            return nothing

        return turn, close, lambda: lax.fori_loop(0, count, sent, 0)

    turn, close, finish_first = relay(0, c1_ref, cs1_ref, e1_ref, False)
    sweep(x_ref, 5, False, turn, e1_ref, complete)
    close()
    rest_second = exchange(y_ref, 1, (0.0,) * 3, ((old_ref, 0, 0, 0, 3),))
    turn, close, finish_second = relay(1, c2_ref, cs2_ref, e2_ref, True)
    sweep(y_ref, 0, True, turn, e2_ref, rest_second)

    loads[7].wait()
    weight = 0.5 * x_ref[1, mine, :span] / x_ref[0, mine, :span]
    term = jnp.zeros((rows, span), jnp.float32)
    for f in range(4):
        if f < 2:
            v = acc_ref[f, mine, :]
            mid = (v + pltpu.roll(v, wid - 1, 1))[:, :span]
        else:
            v = acc_ref[f, pl.ds(WIDE, rows + TILE), :span]
            mid = (v + pltpu.roll(v, rows + TILE - 1, 0))[:rows]
        flow = flow_ref[f]
        if span > cols:
            flow = jnp.concatenate([flow, jnp.zeros((rows, span - cols), jnp.float32)], axis=1)
        term = term + flow * mid
    term_ref[...] = weight * term

    close()
    grad_ref[...] = tot_ref[:, :cols] * (1.0 / (n * STEPS))
    settle()
    finish_first()
    finish_second()


def shards(
    sizes, depth_class, ocean_mask, depth_levels, drag, tide_force, forward_flow, guess
):
    n = sizes[0]
    rows, cols = ocean_mask.shape
    high = rows + 2 * WIDE
    wid = -(-(cols + 2 * WIDE) // LANES) * LANES
    span = -(-cols // LANES) * LANES
    count = rows // TILE
    assert n % 2 == 0 and count > EARLY and rows % TILE == 0 and rows >= WIDE and wid - LANES <= cols
    counts = np.arange(1, n * STEPS + 1)
    angle = 2.0 * math.pi * counts / (n * STEPS)
    trig = jnp.asarray(np.stack([np.cos(angle), np.sin(angle)], axis=1).reshape(-1), jnp.float32)
    f32 = jnp.float32
    vmem = pl.BlockSpec(memory_space=pltpu.VMEM)
    dma = pltpu.SemaphoreType.DMA
    return pl.pallas_call(
        functools.partial(kernel, sizes),
        out_shape=(
            jax.ShapeDtypeStruct((1, 3, rows, cols), f32),
            jax.ShapeDtypeStruct((rows, cols), f32),
        ),
        in_specs=[pl.BlockSpec(memory_space=pl.ANY)] * 8,
        out_specs=(vmem, vmem),
        scratch_shapes=[
            pltpu.VMEM((rows, cols), jnp.int32),
            pltpu.VMEM((rows, cols), jnp.int32),
            pltpu.SMEM(depth_levels.shape, f32),
            pltpu.VMEM((rows, cols), f32),
            pltpu.VMEM(tide_force.shape, f32),
            pltpu.VMEM(forward_flow.shape, f32),
            pltpu.VMEM(guess.shape, f32),
            pltpu.SMEM(trig.shape, f32),
            dma((8,)),
            pltpu.VMEM((8, high, wid), f32),
            pltpu.VMEM((3, high, wid), f32),
            pltpu.VMEM((3, high - EARLY * TILE, wid), f32),
            pltpu.VMEM((3, rows, span), f32),
            pltpu.VMEM((9, high, wid), f32),
            pltpu.VMEM((4, high, wid), f32),
            pltpu.VMEM((3, rows, span), f32),
            pltpu.VMEM((3, rows, span), f32),
            pltpu.VMEM((rows, span), f32),
            pltpu.VMEM((2, rows, LANES), f32),
            pltpu.VMEM((2, rows, LANES), f32),
            pltpu.VMEM((2, high, LANES), f32),
            pltpu.VMEM((2, high, LANES), f32),
            pltpu.VMEM((3, rows, span), f32),
            pltpu.VMEM((3, rows, span), f32),
            pltpu.VMEM((3, rows, span), f32),
            pltpu.VMEM((3, rows, span), f32),
            pltpu.VMEM((3, rows, span), f32),
            pltpu.VMEM((3, rows, span), f32),
            pltpu.VMEM((rows, span), f32),
            pltpu.VMEM((rows, span), f32),
            pltpu.VMEM((rows, span), f32),
            dma((8,)), dma((8,)), dma((16,)), dma((16,)),
            dma((2, count)), dma((2, count)), dma((2, count)), dma((2, count)),
            dma((3,)), dma((3,)),
        ],
        compiler_params=pltpu.CompilerParams(
            collective_id=0, has_side_effects=True, vmem_limit_bytes=56 * 1024 * 1024
        ),
        name="parareal",
    )(depth_class, ocean_mask, depth_levels, drag, tide_force, forward_flow, guess, trig)


def solution(mesh):
    sizes = tuple(mesh.shape[axis] for axis in ("tm", "lat", "lon"))
    return jax.shard_map(
        functools.partial(shards, sizes),
        mesh=mesh,
        in_specs=(
            P("lat", "lon"),
            P("lat", "lon"),
            P(),
            P("lat", "lon"),
            P(None, "lat", "lon"),
            P(None, "lat", "lon"),
            P("tm", None, "lat", "lon"),
        ),
        out_specs=(P("tm", None, "lat", "lon"), P("lat", "lon")),
        check_vma=False,
    )
```
